32 devices in a mesh: scen: 8 (over y, x, core), space: 2 (over z_hi), tm: 2 (over z_lo).
Axes of the slice: x: 2, y: 2, z: 4 (z_hi: 2, z_lo: 2; z = z_hi * 2 + z_lo), core: 2. Of those that a mesh axis runs over, the one named last changes fastest.
Arguments:
- coupling: bfloat16 [8, 4, 2, 128, 512], P('scen', 'tm', 'space'), may hold values from -0.1875 to 0.1875
- leaf_rhs: float32 [8, 4, 2, 128], P('scen', 'tm', 'space'), may hold values from -6 to 6
- conductance: float32 [8, 4, 2, 128], P('scen', 'tm', 'space'), may hold values from 0.42 to 0.52
- compressor: int32 [8, 4, 2], P('scen', 'tm', 'space'), may hold values 0 or 1
- blocks: float32 [8, 4, 2, 128, 128], P('scen', 'tm', 'space'), may hold values from -2 to 8, as said below
- parent_of: int32 [8], P('scen'), may hold values from 0 to 7, as said below
- parent_mat: float32 [8, 512, 512], P(None, ('space', 'tm')), may hold values from -2 to 8, as said below
- parent_rhs: float32 [8, 512], P(None, ('space', 'tm')), may hold values from -6 to 6
- link: float32 [8, 512, 256], P(None, ('space', 'tm')), may hold values from -0.25 to 0.25
- root_mat: float32 [256, 256], replicated, may hold values from -2 to 8, as said below
- root_rhs: float32 [256], replicated, may hold values from -6 to 6
Outputs:
- leaf_move: float32 [8, 4, 2, 128], P('scen', 'tm', 'space')
- parent_at_leaf: float32 [8, 512], P('scen', ('space', 'tm'))
- root_step: float32 [256], replicated
The draws below stay inside these ranges and needn't reach their ends.
Inputs may be any that keep to these rules, and one draw needn't show every extreme that they name: `parent_of`: leaves come in aligned runs of 1 in a row; all leaves of a run share one parent, and each parent owns exactly one run. `blocks`: each block is symmetric with eigenvalues of 1 or more. `parent_mat`: each matrix is symmetric with eigenvalues of 1 or more. `root_mat`: symmetric with eigenvalues of 1 or more.
All inputs are finite; a program needn't handle non-finite values. No bound on the sum of `compressor` on one device may be relied on, other than what follows from the above.
Results may differ from the reference program's by a relative error of at most 0.0003.
Values sent between devices are 32-bit elements; how exact they have to be, the bound alone decides.
A program may use at most 64 MiB of HBM per device.

```python
import jax
import jax.numpy as jnp
from jax import lax

PB = 128
NC = 512
NR = 256
PARENTS = 8
ITERS = 6
LEAVES = 8
NT = 4
NS = 2


def symmetric_gram(key, shape, order):
    base = jax.random.normal(key, shape, jnp.float32)
    return jnp.einsum('...ij,...kj->...ik', base, base) / order


def draw_blocks(key, part):
    gram = symmetric_gram(key, (LEAVES, NT, NS, PB, PB), 4.0 * PB)
    return gram + jnp.eye(PB, dtype=jnp.float32)


def draw_parent_of(key, part):
    order = jax.random.permutation(key, PARENTS)
    return order[jnp.arange(LEAVES) // (LEAVES // PARENTS)].astype(jnp.int32)


def draw_parent_mat(key, part):
    gram = symmetric_gram(key, (PARENTS, NC, NC), 1.0 * NC)
    return gram + jnp.eye(NC, dtype=jnp.float32)


def draw_root_mat(key, part):
    gram = symmetric_gram(key, (NR, NR), 1.0 * NR)
    return gram + jnp.eye(NR, dtype=jnp.float32)


def with_ends(result, key, least, largest):
    index_at = [jax.random.randint(jax.random.fold_in(key, axis), (), 0, length) for axis, length in enumerate(result.shape)]
    widest = result.shape.index(max(result.shape))
    next_to = index_at[:widest] + [(index_at[widest] + 1) % result.shape[widest]] + index_at[widest + 1:]
    return result.at[tuple(index_at)].set(least).at[tuple(next_to)].set(largest)


def level_of(rng, extent, split, low, high):
    gain, own = 1.0, jax.random.fold_in(rng, 6)
    for axis_at, blocks in split:
        draws = jnp.exp(jax.random.uniform(jax.random.fold_in(own, axis_at), (blocks,), jnp.float32, low / len(split), high / len(split)))
        gain = gain * jnp.repeat(draws, extent[axis_at] // blocks).reshape([-1 if axis == axis_at else 1 for axis in range(len(extent))])
    return gain


def bell_draw(rng, shape, spread, limit, shards=(), kind=jnp.bfloat16):
    drawn = jax.random.normal(rng, shape, jnp.float32) * spread
    if len(shards) > 0:
        drawn = level_of(rng, shape, shards, -0.22, 0.18) * drawn
    return jnp.clip(drawn, min=-limit, max=limit).astype(kind)


def setup_inputs(seed: int = 0) -> dict:
    key_of = jax.random.split(jax.random.key(seed), 12)
    coupling = bell_draw(key_of[0], (LEAVES, NT, NS, PB, NC), (NT * NS * PB) ** -0.5, 0.1875, ((0, 8), (1, 2), (2, 2)))
    leaf_rhs = bell_draw(key_of[1], (LEAVES, NT, NS, PB), 1.0, 6.0, ((0, 8), (1, 2), (2, 2)), jnp.float32)
    conductance = jnp.clip(0.42 + 0.099999994 * jax.random.uniform(key_of[2], (LEAVES, NT, NS, PB), jnp.float32) ** level_of(key_of[2], (LEAVES, NT, NS, PB), ((0, 8), (1, 2), (2, 2)), -0.2, 0.2), 0.42, 0.52)
    compressor = with_ends((jax.random.randint(key_of[3], (LEAVES, NT, NS), 0, 4) < 3).astype(jnp.int32), jax.random.fold_in(key_of[3], 1), 0, 1)
    blocks = draw_blocks(jax.random.fold_in(key_of[11], 71), 0)
    parent_of = draw_parent_of(jax.random.fold_in(key_of[11], 71), 0)
    parent_mat = draw_parent_mat(jax.random.fold_in(key_of[11], 71), 0)
    parent_rhs = bell_draw(key_of[7], (PARENTS, NC), 1.0, 6.0, ((1, 4),), jnp.float32)
    link = bell_draw(key_of[8], (PARENTS, NC, NR), NC ** -0.5, 0.25, ((1, 4),), jnp.float32)
    root_mat = draw_root_mat(jax.random.fold_in(key_of[11], 71), 0)
    root_rhs = bell_draw(key_of[10], (NR,), 1.0, 6.0, (), jnp.float32)
    return dict(coupling=coupling, leaf_rhs=leaf_rhs, conductance=conductance, compressor=compressor, blocks=blocks, parent_of=parent_of, parent_mat=parent_mat, parent_rhs=parent_rhs, link=link, root_mat=root_mat, root_rhs=root_rhs)


HIGH = lax.Precision.HIGHEST

def factor_solve(matrix, right):
    factor = lax.linalg.cholesky(matrix)
    forward = lax.linalg.triangular_solve(factor, right, left_side=True, lower=True)
    return lax.linalg.triangular_solve(factor, forward, left_side=True, lower=True, transpose_a=True)

def invert_blocks(matrices):
    identity = jnp.broadcast_to(jnp.eye(matrices.shape[-1], dtype=matrices.dtype), matrices.shape)
    return factor_solve(matrices, identity)

def beside_all(padded):
    return padded[2:, 1:-1] + padded[:-2, 1:-1] + padded[1:-1, 2:] + padded[1:-1, :-2]

def couple(field, weight):
    scale = weight
    if field.ndim == 4:
        scale = weight[..., None]
    widths = [(1, 1), (1, 1)] + [(0, 0)] * (field.ndim - 2)
    return beside_all(jnp.pad(field * scale, widths)) * scale

def block_apply(inverse, field):
    if field.ndim == 4:
        return jnp.einsum('tsij,tsjc->tsic', inverse, field, precision=HIGH)
    return jnp.einsum('tsij,tsj->tsi', inverse, field, precision=HIGH)

def jacobi(source, inverse, weight):
    field = block_apply(inverse, source)
    for sweep_index in range(ITERS - 1):
        field = block_apply(inverse, source + couple(field, weight))
    return field

def reference(coupling, leaf_rhs, conductance, compressor, blocks, parent_of, parent_mat, parent_rhs, link, root_mat, root_rhs):
    weight = conductance * (1.0 + compressor.astype(jnp.float32)[..., None]) * 0.5
    inverse = invert_blocks(blocks)

    def leaf_terms(leaf_items):
        dense, right, leaf_weight, leaf_inverse = leaf_items
        dense = dense.astype(jnp.float32)
        solved = jacobi(dense, leaf_inverse, leaf_weight)
        pulled = jacobi(right, leaf_inverse, leaf_weight)
        schur = jnp.einsum('tsic,tsid->cd', dense, solved, precision=HIGH)
        gather_term = jnp.einsum('tsic,tsi->c', dense, pulled, precision=HIGH)
        return (schur, gather_term)
    schur, pulled = lax.map(leaf_terms, (coupling, leaf_rhs, weight, inverse))
    onehot = (parent_of[:, None] == jnp.arange(PARENTS, dtype=jnp.int32)[None, :]).astype(jnp.float32)
    hessian = parent_mat + jnp.einsum('lp,lij->pij', onehot, schur, precision=HIGH)
    reduced = jnp.einsum('lp,li->pi', onehot, pulled, precision=HIGH) - parent_rhs
    link_solved = factor_solve(hessian, link)
    vector_solved = factor_solve(hessian, reduced[..., None])[..., 0]
    root_matrix = root_mat + jnp.einsum('pin,pim->nm', link, link_solved, precision=HIGH)
    root_right = root_rhs - jnp.einsum('pin,pi->n', link, vector_solved, precision=HIGH)
    root_step = factor_solve(root_matrix, root_right[:, None])[:, 0]
    parent_step = vector_solved + jnp.einsum('pin,n->pi', link_solved, root_step, precision=HIGH)
    parent_at_leaf = jnp.einsum('lp,pi->li', onehot, parent_step, precision=HIGH)

    def leaf_step(leaf_items):
        dense, right, leaf_weight, leaf_inverse, target = leaf_items
        source = right - jnp.einsum('tsic,c->tsi', dense.astype(jnp.float32), target, precision=HIGH)
        return jacobi(source, leaf_inverse, leaf_weight)
    leaf_move = lax.map(leaf_step, (coupling, leaf_rhs, weight, inverse, parent_at_leaf))
    return (leaf_move, parent_at_leaf, root_step)
```

```python
import functools

import jax
import jax.numpy as jnp
from jax import lax
from jax.experimental import pallas as pl
from jax.experimental.pallas import tpu as pltpu
from jax.sharding import PartitionSpec as P

PARENTS = 8
ITERS = 6
LANES = 128
F32 = jnp.float32
BF16 = jnp.bfloat16
HIGH = lax.Precision.HIGHEST
MESH = pl.DeviceIdType.MESH
VMEM = pl.BlockSpec(memory_space=pltpu.VMEM)
ANY = pl.BlockSpec(memory_space=pl.ANY)
LIMIT = 56 * 1024 * 1024
SETTLED = 1e-7
NN = ((1,), (0,))
NT = ((1,), (1,))
TN = ((0,), (0,))


def full_dot(a, b, dims=NN):
    return lax.dot_general(a, b, (dims, ((), ())), precision=HIGH, preferred_element_type=F32)


def fast_dot(a, b, dims=NN):
    return lax.dot_general(a, b, (dims, ((), ())), preferred_element_type=F32)


def halves(x):
    top = x.astype(BF16)
    return top, (x - top.astype(F32)).astype(BF16)


def as_columns(row):
    return jnp.broadcast_to(row, (LANES, LANES)).T


def spd_inverses(matrices):
    size = matrices[0].shape[0]
    row = lax.broadcasted_iota(jnp.int32, (size, size), 0)
    column = lax.broadcasted_iota(jnp.int32, (size, size), 1)
    identity = jnp.where(row == column, 1.0, 0.0).astype(F32)
    rho = None
    pairs = []
    for matrix in matrices:
        square = full_dot(matrix, matrix)
        plain = jnp.max(jnp.sum(jnp.abs(matrix), axis=0, keepdims=True), axis=1, keepdims=True)
        squared = jnp.max(jnp.sum(jnp.abs(square), axis=0, keepdims=True), axis=1, keepdims=True)
        bound = jnp.maximum(jnp.minimum(plain, jnp.sqrt(squared)) * 1.0001, 1.0)
        total, spread = bound + 1.0, bound - 1.0
        scale = 1.0 / (2.0 * total * total - spread * spread)
        alpha, beta = 8.0 * total * scale, 8.0 * scale
        start = alpha * identity - beta * matrix
        residual = identity - alpha * matrix + beta * square
        pairs.append((start, residual))
        own = jnp.max(spread * spread * scale)
        rho = own if rho is None else jnp.maximum(rho, own)

    def more(state):
        return (state[0] > SETTLED) & (state[1] < 32)

    def step(state):
        norm, count, items = state
        after = []
        for x, r in items:
            both = full_dot(jnp.concatenate([x, r], axis=0), r)
            after.append((x + both[:size], both[size:]))
        return norm * norm, count + 1, after

    return [x for x, _ in lax.while_loop(more, step, (rho, jnp.int32(0), pairs))[2]]


def block_kernel(blocks_ref, inverse_ref):
    count, size, _ = blocks_ref.shape
    zero = jnp.zeros((size, size), F32)
    for i in range(0, count, 2):
        j = min(i + 1, count - 1)
        pair = jnp.concatenate(
            [
                jnp.concatenate([blocks_ref[i], zero], axis=1),
                jnp.concatenate([zero, blocks_ref[j]], axis=1),
            ],
            axis=0,
        )
        found = spd_inverses([pair])[0]
        inverse_ref[i] = found[:size, :size]
        inverse_ref[j] = found[size:, size:]


def leaf_kernel(beside, per, coupling_ref, inverse_ref, vector_ref, schur_ref, solved_ref,
                field, plain, scaled, weight_ref, bits):
    count = len(beside)
    columns = coupling_ref.shape[-1]
    wide = columns + LANES

    def stacked(matrix):
        top, low = halves(matrix)
        return jnp.concatenate([top, low, top], axis=1)

    def stack(x):
        top, low = halves(x)
        return jnp.concatenate([top, top, low], axis=0)

    def source(n, start, width):
        g, k = divmod(n, per)
        parts = []
        if start < columns:
            parts.append(coupling_ref[g, k, :, pl.ds(start, min(width, columns - start))])
        if start + width > columns:
            parts.append(as_columns(vector_ref[g, k:k + 1, :]))
        return jnp.concatenate(parts, axis=1)

    for n in range(count):
        g, k = divmod(n, per)
        weight_row = vector_ref[g, per + k:per + k + 1, :]
        weight = as_columns(weight_row)
        inverse = inverse_ref[g, k]
        weight_ref[n] = weight
        plain[n] = stacked(inverse)
        scaled[n] = stacked(weight * inverse * weight_row)
        bits[pl.ds(n * LANES, LANES), :] = coupling_ref[g, k].astype(BF16)

    def around(slot, n):
        total = field[slot, beside[n][0]]
        for m in beside[n][1:]:
            total = total + field[slot, m]
        return total

    width = field.shape[-1]
    last = (ITERS - 2) % 2
    for start in range(0, wide, width):
        here = pl.ds(start, width)

        def spread(n):
            return jnp.concatenate([weight_ref[n]] * (width // LANES), axis=1)

        for n in range(count):
            first = spread(n) * fast_dot(plain[n], stack(source(n, start, width)))
            field[0, n] = first
            solved_ref[n, :, here] = first

        def sweep(k, carry):
            now = lax.rem(k, 2)
            for n in range(count):
                moved = fast_dot(scaled[n], stack(around(now, n)))
                field[1 - now, n] = solved_ref[n, :, here] + moved
            return carry

        lax.fori_loop(0, ITERS - 2, sweep, 0)
        for n in range(count):
            drive = source(n, start, width) + spread(n) * around(last, n)
            solved_ref[n, :, here] = fast_dot(plain[n], stack(drive))
    chunk = min(count, 8)
    for c in range(0, count, chunk):
        top, low = halves(solved_ref[pl.ds(c, chunk)].reshape(chunk * LANES, wide))
        own = bits[pl.ds(c * LANES, chunk * LANES), :]
        part = fast_dot(own, top, TN) + fast_dot(own, low, TN)
        schur_ref[...] = part if c == 0 else schur_ref[...] + part


def parent_kernel(schur_ref, matrix_ref, right_ref, link_ref, solution_ref, term_ref):
    size = matrix_ref.shape[0]
    half = size // 2
    roots = link_ref.shape[1]
    wide = roots + LANES
    right = jnp.concatenate(
        [as_columns(right_ref[:, pl.ds(c, LANES)]) for c in range(0, size, LANES)], axis=0
    )
    sides = jnp.concatenate([link_ref[...], schur_ref[:, pl.ds(size, LANES)] - right], axis=1)
    a, b = pl.ds(0, half), pl.ds(half, half)
    h11 = matrix_ref[a, a] + schur_ref[a, a]
    h12 = matrix_ref[a, b] + schur_ref[a, b]
    h21 = matrix_ref[b, a] + schur_ref[b, a]
    h22 = matrix_ref[b, b] + schur_ref[b, b]
    x11 = spd_inverses([h11])[0]
    eliminated = full_dot(x11, jnp.concatenate([h12, sides[:half]], axis=1))
    rest = full_dot(h21, eliminated)
    x22 = spd_inverses([h22 - rest[:, :half]])[0]
    lower = full_dot(x22, sides[half:] - rest[:, half:])
    upper = eliminated[:, half:] - full_dot(eliminated[:, :half], lower)
    solution_ref[a, :] = upper
    solution_ref[b, :] = lower
    term_ref[...] = full_dot(solution_ref[...], link_ref[...], TN)[:roots + 8]


def root_kernel(matrix_ref, term_ref, vector_ref, right_ref, solution_ref, solved_ref, pack_ref):
    roots = matrix_ref.shape[0]
    size = solution_ref.shape[0]
    groups = pack_ref.shape[0]
    per = solved_ref.shape[0] // groups
    inverse = spd_inverses([matrix_ref[...] + term_ref[...]])[0]
    root = full_dot(right_ref[...] - vector_ref[...], inverse)
    lane = lax.broadcasted_iota(jnp.int32, (8, LANES), 1)
    unit = jnp.where(lane == 0, 1.0, 0.0).astype(F32)
    parent = full_dot(jnp.concatenate([root, unit], axis=1), solution_ref[...], NT)
    mix = jnp.concatenate([-parent, unit], axis=1)
    for g in range(groups):
        for k in range(per):
            pack_ref[g, :, pl.ds(k * LANES, LANES)] = full_dot(mix, solved_ref[g * per + k], NT)
        pack_ref[g, :, pl.ds(per * LANES, size)] = parent
        pack_ref[g, :, pl.ds(per * LANES + size, roots)] = root


class Plan:
    def __init__(self, mesh):
        self.scen, self.space, self.tm = (mesh.shape[name] for name in ("scen", "space", "tm"))
        self.members = self.space * self.tm
        self.siblings = self.scen // PARENTS

    def leader(self, scen):
        middle = self.members // 2
        if self.siblings == 1:
            return middle - lax.rem(scen, 2)
        return middle + 0 * scen

    def device(self, scen, member):
        return (scen, lax.div(member, self.tm), lax.rem(member, self.tm))

    def here(self):
        return lax.axis_index("scen"), lax.axis_index("space") * self.tm + lax.axis_index("tm")


def gather_kernel(plan, count, *refs):
    sources, targets = refs[:count], refs[count:2 * count]
    send, receive, local = refs[2 * count:]
    scen, member = plan.here()
    lead = plan.leader(scen)
    barrier = pltpu.get_barrier_semaphore()

    def remote(i, place, slot):
        return pltpu.make_async_remote_copy(
            src_ref=sources[i], dst_ref=targets[i].at[place], send_sem=send.at[i],
            recv_sem=receive.at[i, slot], device_id=plan.device(scen, lead), device_id_type=MESH,
        )

    @pl.when(member != lead)
    def _():
        pl.semaphore_signal(barrier, inc=1, device_id=plan.device(scen, lead), device_id_type=MESH)
        pl.semaphore_wait(barrier, 1)
        slot = lax.rem(member - lead + plan.members, plan.members) - 1
        copies = [remote(i, member, slot) for i in range(count)]
        for copy in copies:
            copy.start()
        for copy in copies:
            copy.wait_send()

    @pl.when(member == lead)
    def _():
        others = [lax.rem(lead + k, plan.members) for k in range(1, plan.members)]
        for other in others:
            pl.semaphore_signal(
                barrier, inc=1, device_id=plan.device(scen, other), device_id_type=MESH
            )
        own = [pltpu.make_async_copy(sources[i], targets[i].at[member], local.at[i]) for i in range(count)]
        for copy in own:
            copy.start()
        pl.semaphore_wait(barrier, plan.members - 1)
        for slot, other in enumerate(others):
            for i in range(count):
                remote(i, other, slot).wait_recv()
        for copy in own:
            copy.wait()


def gather(plan, arrays):
    count = len(arrays)
    return pl.pallas_call(
        functools.partial(gather_kernel, plan, count),
        out_shape=[jax.ShapeDtypeStruct((plan.members,) + x.shape, x.dtype) for x in arrays],
        in_specs=[ANY] * count,
        out_specs=[ANY] * count,
        scratch_shapes=[
            pltpu.SemaphoreType.DMA((count,)),
            pltpu.SemaphoreType.DMA((count, plan.members - 1)),
            pltpu.SemaphoreType.DMA((count,)),
        ],
        compiler_params=pltpu.CompilerParams(collective_id=0, has_side_effects=True),
    )(*arrays)


def sum_kernel(plan, term_ref, total_ref, vector_ref, strips, vectors, whole,
               send, receive):
    scen, member = plan.here()
    lead = plan.leader(scen)
    count = plan.scen
    roots = whole.shape[0]
    rows = roots // count
    barrier = pltpu.get_barrier_semaphore()

    @pl.when(member == lead)
    def _():
        peers = [lax.rem(scen + k, count) for k in range(1, count)]
        devices = [plan.device(peer, plan.leader(peer)) for peer in peers]
        for device in devices:
            pl.semaphore_signal(barrier, inc=1, device_id=device, device_id_type=MESH)
        mine = pl.ds(pl.multiple_of(scen * rows, rows), rows)
        strips[scen] = term_ref[mine, :]
        vectors[scen] = term_ref[pl.ds(roots, 8), :]
        pl.semaphore_wait(barrier, count - 1)

        def remote(kind, k, source, target):
            return pltpu.make_async_remote_copy(
                src_ref=source, dst_ref=target, send_sem=send.at[kind, k],
                recv_sem=receive.at[kind, k], device_id=devices[k], device_id_type=MESH,
            )

        copies = []
        for k, peer in enumerate(peers):
            theirs = pl.ds(pl.multiple_of(peer * rows, rows), rows)
            copies.append(remote(0, k, term_ref.at[theirs, :], strips.at[scen]))
            copies.append(remote(1, k, term_ref.at[pl.ds(roots, 8), :], vectors.at[scen]))
        for copy in copies:
            copy.start()
        for copy in copies:
            copy.wait()
        total = strips[0]
        vector = vectors[0]
        for s in range(1, count):
            total = total + strips[s]
            vector = vector + vectors[s]
        vector_ref[...] = vector
        whole[mine, :] = total
        copies = [remote(2, k, whole.at[mine, :], whole.at[mine, :]) for k in range(count - 1)]
        for copy in copies:
            copy.start()
        for copy in copies:
            copy.wait()
        total_ref[...] = whole[...]

    @pl.when(member != lead)
    def _():
        total_ref[...] = jnp.zeros_like(total_ref)
        vector_ref[...] = jnp.zeros_like(vector_ref)


def sum_terms(plan, term):
    roots = term.shape[1]
    return pl.pallas_call(
        functools.partial(sum_kernel, plan),
        out_shape=[jax.ShapeDtypeStruct((roots, roots), F32), jax.ShapeDtypeStruct((8, roots), F32)],
        in_specs=[VMEM],
        out_specs=[VMEM] * 2,
        scratch_shapes=[
            pltpu.VMEM((plan.scen, roots // plan.scen, roots), F32),
            pltpu.VMEM((plan.scen, 8, roots), F32),
            pltpu.VMEM((roots, roots), F32),
            pltpu.SemaphoreType.DMA((3, plan.scen - 1)),
            pltpu.SemaphoreType.DMA((3, plan.scen - 1)),
        ],
        compiler_params=pltpu.CompilerParams(collective_id=1, has_side_effects=True),
    )(term)


def scatter_kernel(plan, pack_ref, out_ref, landed, send, receive):
    scen, member = plan.here()
    lead = plan.leader(scen)
    barrier = pltpu.get_barrier_semaphore()

    def remote(k, other):
        return pltpu.make_async_remote_copy(
            src_ref=pack_ref.at[other], dst_ref=landed, send_sem=send.at[k],
            recv_sem=receive, device_id=plan.device(scen, other), device_id_type=MESH,
        )

    @pl.when(member != lead)
    def _():
        pl.semaphore_signal(barrier, inc=1, device_id=plan.device(scen, lead), device_id_type=MESH)
        pl.semaphore_wait(barrier, 1)
        remote(0, lead).wait_recv()
        out_ref[...] = landed[...]

    @pl.when(member == lead)
    def _():
        others = [lax.rem(lead + k, plan.members) for k in range(1, plan.members)]
        for other in others:
            pl.semaphore_signal(
                barrier, inc=1, device_id=plan.device(scen, other), device_id_type=MESH
            )
        pl.semaphore_wait(barrier, plan.members - 1)
        copies = [remote(k, other) for k, other in enumerate(others)]
        for copy in copies:
            copy.start()
        out_ref[...] = pack_ref[member]
        for copy in copies:
            copy.wait_send()


def scatter(plan, pack):
    return pl.pallas_call(
        functools.partial(scatter_kernel, plan),
        out_shape=jax.ShapeDtypeStruct(pack.shape[1:], F32),
        in_specs=[VMEM],
        out_specs=VMEM,
        scratch_shapes=[
            pltpu.VMEM(pack.shape[1:], F32),
            pltpu.SemaphoreType.DMA((plan.members - 1,)),
            pltpu.SemaphoreType.DMA,
        ],
        compiler_params=pltpu.CompilerParams(collective_id=2, has_side_effects=True),
    )(pack)


def local_call(kernel, out_shape, count, scratch=()):
    many = isinstance(out_shape, list)
    return pl.pallas_call(
        kernel,
        out_shape=out_shape,
        in_specs=[VMEM] * count,
        out_specs=[VMEM] * len(out_shape) if many else VMEM,
        scratch_shapes=list(scratch),
        compiler_params=pltpu.CompilerParams(vmem_limit_bytes=LIMIT),
    )


def from_partner(block, axis, bit):
    count = lax.axis_size(axis)
    route = []
    for low in range(count):
        high = low | 1 << bit
        if high != low and high < count:
            route += [(low, high), (high, low)]
    return lax.ppermute(block, axis, route)


def neighbours(plan, times, cells):
    place = {}
    for g in range(plan.members):
        for t in range(times):
            for s in range(cells):
                at = ((g % plan.tm) * times + t, (g // plan.tm) * cells + s)
                place[at] = (g * times + t) * cells + s
    found = [None] * len(place)
    for (t, s), n in place.items():
        sides = [(t + 1, s), (t - 1, s), (t, s + 1), (t, s - 1)]
        found[n] = [place[side] for side in sides if side in place]
    return found


def body(
    plan,
    coupling,
    leaf_rhs,
    conductance,
    compressor,
    blocks,
    parent_of,
    parent_mat,
    parent_rhs,
    link,
    root_mat,
    root_rhs,
):
    _, times, cells, rows, size = coupling.shape
    per = times * cells
    roots = root_rhs.shape[0]
    share = parent_rhs.shape[1]
    count = plan.members * per
    dense = coupling.reshape(per, rows, size).astype(F32)
    weight = conductance[0] * (1.0 + compressor[0].astype(F32)[..., None]) * 0.5
    inverse = local_call(block_kernel, jax.ShapeDtypeStruct((per, rows, rows), F32), 1)(
        blocks.reshape(per, rows, rows)
    )
    label = parent_of[0]
    own_mat = lax.dynamic_index_in_dim(parent_mat, label, 0, keepdims=False)
    own_rhs = lax.dynamic_index_in_dim(parent_rhs, label, 0, keepdims=True)
    own_link = lax.dynamic_index_in_dim(link, label, 0, keepdims=False)
    lines = jnp.concatenate(
        [
            leaf_rhs.reshape(per, rows),
            weight.reshape(per, rows),
            jnp.pad(own_rhs, ((0, 0), (0, LANES - share))),
        ],
        axis=0,
    )
    lines = jnp.pad(lines, ((0, -lines.shape[0] % 8), (0, 0)))
    all_dense, all_inverse, all_mat, all_link, all_lines = gather(
        plan, [dense, inverse, own_mat, own_link, lines]
    )
    wide = size + LANES
    schur, solved = local_call(
        functools.partial(leaf_kernel, neighbours(plan, times, cells), per),
        [jax.ShapeDtypeStruct((size, wide), F32), jax.ShapeDtypeStruct((count, rows, wide), F32)],
        3,
        [
            pltpu.VMEM((2, count, rows, wide if count <= 8 else LANES), F32),
            pltpu.VMEM((count, rows, 3 * rows), BF16),
            pltpu.VMEM((count, rows, 3 * rows), BF16),
            pltpu.VMEM((count, rows, LANES), F32),
            pltpu.VMEM((count * rows, size), BF16),
        ],
    )(all_dense, all_inverse, all_lines)
    for bit_index in range(plan.siblings.bit_length() - 1):
        schur = schur + from_partner(schur, "scen", bit_index)
    right = all_lines[:, 2 * per, :share].reshape(1, size)
    solution_p, term = local_call(
        parent_kernel,
        [
            jax.ShapeDtypeStruct((size, roots + LANES), F32),
            jax.ShapeDtypeStruct((roots + 8, roots), F32),
        ],
        4,
    )(schur, all_mat.reshape(size, size), right, all_link.reshape(size, roots))
    if plan.siblings > 1:
        term = jnp.where(lax.axis_index("scen") % plan.siblings == 0, term, 0.0)
    total, vector = sum_terms(plan, term)
    pack = local_call(
        root_kernel,
        jax.ShapeDtypeStruct((plan.members, 8, per * rows + size + roots), F32),
        6,
    )(root_mat, total, vector, root_rhs[None], solution_p, solved)
    line = scatter(plan, pack)[0]
    leaf_move = line[: per * rows].reshape(leaf_rhs.shape)
    strip = lax.axis_index("space") * plan.tm + lax.axis_index("tm")
    parent_at_leaf = lax.dynamic_slice_in_dim(line, per * rows + strip * share, share)[None]
    return leaf_move, parent_at_leaf, line[per * rows + size :]


def solution(mesh):
    return jax.shard_map(
        functools.partial(body, Plan(mesh)),
        mesh=mesh,
        in_specs=(
            P("scen", "tm", "space", None, None),
            P("scen", "tm", "space", None),
            P("scen", "tm", "space", None),
            P("scen", "tm", "space"),
            P("scen", "tm", "space", None, None),
            P("scen"),
            P(None, ("space", "tm"), None),
            P(None, ("space", "tm")),
            P(None, ("space", "tm"), None),
            P(),
            P(),
        ),
        out_specs=(P("scen", "tm", "space", None), P("scen", ("space", "tm")), P()),
        check_vma=False,
    )
```

```python
import functools

import jax
import jax.numpy as jnp
from jax import lax
from jax.experimental import pallas as pl
from jax.experimental.pallas import tpu as pltpu
from jax.sharding import PartitionSpec as P

PARENTS = 8
ITERS = 6
LANES = 128
F32 = jnp.float32
BF16 = jnp.bfloat16
HIGH = lax.Precision.HIGHEST
MESH = pl.DeviceIdType.MESH
VMEM = pl.BlockSpec(memory_space=pltpu.VMEM)
ANY = pl.BlockSpec(memory_space=pl.ANY)
LIMIT = 56 * 1024 * 1024
SETTLED = 3e-4
NN = ((1,), (0,))
NT = ((1,), (1,))
TN = ((0,), (0,))


def full_dot(a, b, dims=NN):
    return lax.dot_general(a, b, (dims, ((), ())), precision=HIGH, preferred_element_type=F32)


def fast_dot(a, b, dims=NN):
    return lax.dot_general(a, b, (dims, ((), ())), preferred_element_type=F32)


def halves(x):
    top = x.astype(BF16)
    return top, (x - top.astype(F32)).astype(BF16)


def as_columns(row):
    return jnp.broadcast_to(row, (LANES, LANES)).T


def near_dot(a, b, dims=NN):
    a_top, a_low = halves(a)
    b_top, b_low = halves(b)
    return fast_dot(a_top, b_top, dims) + fast_dot(a_top, b_low, dims) + fast_dot(a_low, b_top, dims)


def spd_inverse(matrix, steps=None):
    size = matrix.shape[0]
    row = lax.broadcasted_iota(jnp.int32, (size, size), 0)
    column = lax.broadcasted_iota(jnp.int32, (size, size), 1)
    identity = jnp.where(row == column, 1.0, 0.0).astype(F32)
    square = near_dot(matrix, matrix)
    plain = jnp.max(jnp.sum(jnp.abs(matrix), axis=0, keepdims=True), axis=1, keepdims=True)
    squared = jnp.max(jnp.sum(jnp.abs(square), axis=0, keepdims=True), axis=1, keepdims=True)
    bound = jnp.maximum(jnp.minimum(plain, jnp.sqrt(squared)) * 1.0001, 1.0)
    total, spread = bound + 1.0, bound - 1.0
    scale = 1.0 / (2.0 * total * total - spread * spread)
    alpha, beta = 8.0 * total * scale, 8.0 * scale
    start = alpha * identity - beta * matrix
    residual = identity - alpha * matrix + beta * square

    def grow(x, r):
        both = near_dot(jnp.concatenate([x, r], axis=0), r)
        return x + both[:size], both[size:]

    def correct(_, x):
        return x + near_dot(x, identity - full_dot(matrix, x))

    if steps is not None:
        x, _ = lax.fori_loop(0, steps, lambda _, state: grow(*state), (start, residual))
        return lax.fori_loop(0, 2, correct, x)
    rho = jnp.max(spread * spread * scale)
    largest = jnp.max(bound)
    _, _, x, _ = lax.while_loop(
        lambda state: (state[0] > SETTLED) & (state[1] < 32),
        lambda state: (state[0] * state[0], state[1] + 1) + grow(*state[2:]),
        (rho, jnp.int32(0), start, residual),
    )
    rounds = 1 + (largest > 50.0).astype(jnp.int32) + (largest > 1000.0).astype(jnp.int32)
    return lax.fori_loop(0, rounds, correct, x)


def steps_for(bound):
    rho = (bound - 1.0) ** 2 / (2.0 * (bound + 1.0) ** 2 - (bound - 1.0) ** 2)
    steps = 0
    while rho > SETTLED:
        rho, steps = rho * rho, steps + 1
    return steps


def parent_kernel(plan, schur_ref, diagonal_ref, beside_ref, right_ref, link_ref, solution_ref, term_ref):
    half = diagonal_ref.shape[1]
    size = 2 * half
    roots = link_ref.shape[1]
    scen, _ = plan.here()
    near = lax.div(plan.leader(scen), plan.members // 2)
    right = jnp.concatenate(
        [as_columns(right_ref[:, pl.ds(c, LANES)]) for c in range(0, size, LANES)], axis=0
    )
    sides = jnp.concatenate([link_ref[...], schur_ref[:, pl.ds(half, LANES)] - right], axis=1)
    a, b = pl.ds(0, half), pl.ds(half, half)
    behind = pl.ds(half + LANES, half)
    beside = beside_ref[...]
    h11 = diagonal_ref[a, :] + schur_ref[a, a]
    h12 = jnp.where(near == 0, beside, beside.T) + schur_ref[a, behind]
    h22 = diagonal_ref[b, :] + schur_ref[b, behind]
    x11 = spd_inverse(h11)
    eliminated = full_dot(x11, jnp.concatenate([h12, sides[:half]], axis=1))
    rest = full_dot(h12, eliminated, TN)
    x22 = spd_inverse(h22 - rest[:, :half])
    lower = near_dot(x22, sides[half:] - rest[:, half:])
    upper = eliminated[:, half:] - near_dot(eliminated[:, :half], lower)
    solution_ref[a, :] = upper
    solution_ref[b, :] = lower
    term_ref[...] = near_dot(solution_ref[...], link_ref[...], TN)[:roots + 8]


def root_kernel(matrix_ref, term_ref, vector_ref, right_ref, solution_ref, solved_ref, pack_ref):
    roots = matrix_ref.shape[0]
    size = solution_ref.shape[0]
    groups = pack_ref.shape[0]
    count, rows, wide = solved_ref.shape
    per = count // groups
    share = size // groups
    inverse = spd_inverse(matrix_ref[...] + term_ref[...])
    root = full_dot(right_ref[...] - vector_ref[...], inverse)
    lane = lax.broadcasted_iota(jnp.int32, (8, LANES), 1)
    unit = jnp.where(lane == 0, 1.0, 0.0).astype(F32)
    parent = full_dot(jnp.concatenate([root, unit], axis=1), solution_ref[...], NT)
    mix = jnp.concatenate([-parent[:, :size // 2], unit, -parent[:, size // 2:]], axis=1)
    for g in range(groups):
        own = solved_ref[pl.ds(g * per, per)].reshape(per * rows, wide)
        pack_ref[g, :, pl.ds(0, per * rows)] = near_dot(mix, own, NT)
        pack_ref[g, :, pl.ds(per * rows, roots)] = root
        pack_ref[g, :, pl.ds(per * rows + roots, share)] = parent[:, g * share:(g + 1) * share]


class Plan:
    def __init__(self, mesh):
        self.scen, self.space, self.tm = (mesh.shape[name] for name in ("scen", "space", "tm"))
        self.members = self.space * self.tm
        self.siblings = self.scen // PARENTS

    def leader(self, scen):
        middle = self.members // 2
        if self.siblings == 1:
            return middle - lax.rem(scen, 2)
        return middle + 0 * scen

    def device(self, scen, member):
        return (scen, lax.div(member, self.tm), lax.rem(member, self.tm))

    def here(self):
        return lax.axis_index("scen"), lax.axis_index("space") * self.tm + lax.axis_index("tm")


def leaf_kernel(plan, beside, per, coupling_ref, rhs_ref, conductance_ref, compressor_ref, blocks_ref,
                parent_of_ref, parent_mat_ref, parent_rhs_ref, link_ref,
                schur_ref, solved_ref, right_ref, all_diagonal, all_beside, all_link,
                own_lines, own_half, own_inverse, own_diagonal, own_beside, own_link,
                all_lines, all_half, all_inverse,
                field, plain, scaled, weight_ref, bits, send, receive, local):
    count = len(beside)
    members = plan.members
    times, cells = coupling_ref.shape[1:3]
    half = coupling_ref.shape[-1] // 2
    share = parent_rhs_ref.shape[1]
    scen, member = plan.here()
    lead = plan.leader(scen)
    leads = member == lead
    close = lax.div(member, members // 2) == lax.div(lead, members // 2)
    place = lax.rem(member, members // 2)
    barrier = pltpu.get_barrier_semaphore()
    LINES, FIRST, INVERSE, SECOND, DIAGONAL, LINK, BESIDE = range(7)

    def remote(kind, at, slot):
        source, target = {
            LINES: (own_lines, all_lines.at[at]),
            FIRST: (own_half.at[0], all_half.at[0, at]),
            INVERSE: (own_inverse, all_inverse.at[at]),
            SECOND: (own_half.at[1], all_half.at[1, at]),
            DIAGONAL: (own_diagonal, all_diagonal.at[at]),
            LINK: (own_link, all_link.at[at]),
            BESIDE: (own_beside, all_beside.at[lax.rem(at, members // 2)]),
        }[kind]
        return pltpu.make_async_remote_copy(
            src_ref=source, dst_ref=target, send_sem=send.at[kind], recv_sem=receive.at[kind, slot],
            device_id=plan.device(scen, lead), device_id_type=MESH,
        )

    others = [lax.rem(lead + k, members) for k in range(1, members)]
    slot = lax.rem(member - lead + members, members) - 1

    @pl.when(leads)
    def _():
        for other in others:
            pl.semaphore_signal(
                barrier, inc=1, device_id=plan.device(scen, other), device_id_type=MESH
            )

    @pl.when(jnp.logical_not(leads))
    def _():
        pl.semaphore_signal(barrier, inc=1, device_id=plan.device(scen, lead), device_id_type=MESH)

    label = parent_of_ref[0]
    own_lines[...] = jnp.zeros_like(own_lines)
    for k in range(per):
        t, c = divmod(k, cells)
        own_lines[k:k + 1, :] = rhs_ref[0, t, c:c + 1, :]
        doubled = 1.0 + compressor_ref[0, t, c].astype(F32)
        own_lines[per + k:per + k + 1, :] = conductance_ref[0, t, c:c + 1, :] * doubled * 0.5
        for j in range(2):
            own_half[j, k] = coupling_ref[0, t, c, :, pl.ds(j * half, half)].astype(F32)
    own_lines[2 * per:2 * per + 1, pl.ds(0, share)] = parent_rhs_ref[pl.ds(label, 1), :]

    @pl.when(jnp.logical_not(leads))
    def _():
        pl.semaphore_wait(barrier, 1)
        remote(LINES, member, slot).start()
        remote(FIRST, member, slot).start()

    rows = blocks_ref.shape[-1]
    zero = jnp.zeros((rows, rows), F32)
    for i in range(0, per, 2):
        j = min(i + 1, per - 1)
        first = blocks_ref[0, i // cells, i % cells]
        second = blocks_ref[0, j // cells, j % cells]
        pair = jnp.concatenate(
            [jnp.concatenate([first, zero], axis=1), jnp.concatenate([zero, second], axis=1)], axis=0
        )
        found = spd_inverse(pair, steps_for(8.0 * rows))
        own_inverse[i] = found[:rows, :rows]
        own_inverse[j] = found[rows:, rows:]
    strip = parent_mat_ref[label]
    lower = lax.div(member, members // 2) == 0
    own_diagonal[...] = jnp.where(lower, strip[:, :half], strip[:, half:])
    own_beside[...] = jnp.where(lower, strip[:, half:], strip[:, :half])
    own_link[...] = link_ref[label]

    @pl.when(jnp.logical_not(leads))
    def _():
        remote(INVERSE, member, slot).start()
        remote(SECOND, member, slot).start()
        for kind in (LINES, FIRST, INVERSE, SECOND):
            remote(kind, member, slot).wait_send()
        remote(DIAGONAL, member, slot).start()
        remote(LINK, member, slot).start()

        @pl.when(close)
        def _():
            remote(BESIDE, member, slot).start()
            remote(BESIDE, member, slot).wait_send()

        remote(DIAGONAL, member, slot).wait_send()
        remote(LINK, member, slot).wait_send()

    def arrived(*kinds):
        for kind in kinds:
            for k, other in enumerate(others):
                remote(kind, other, k).wait_recv()

    def stacked(matrix):
        top, low = halves(matrix)
        return jnp.concatenate([top, low, top], axis=1)

    def stack(x):
        top, low = halves(x)
        return jnp.concatenate([top, top, low], axis=0)

    def source(n, units):
        g, k = divmod(n, per)
        parts = []
        for unit in units:
            if unit is None:
                parts.append(as_columns(all_lines[g, k:k + 1, :]))
            else:
                j, start = divmod(unit, half)
                parts.append(all_half[j, g, k, :, pl.ds(start, LANES)])
        return jnp.concatenate(parts, axis=1)

    def around(at, n):
        total = field[at, beside[n][0]]
        for m in beside[n][1:]:
            total = total + field[at, m]
        return total

    last = (ITERS - 2) % 2

    def solve(units, start):
        width = LANES * len(units)
        here = pl.ds(start, width)

        def spread(n):
            return jnp.concatenate([weight_ref[n]] * len(units), axis=1)

        for n in range(count):
            first = spread(n) * fast_dot(plain[n], stack(source(n, units)))
            field[0, n, :, pl.ds(0, width)] = first
            solved_ref[n, :, here] = first

        def sweep(k, carry):
            now = lax.rem(k, 2)
            for n in range(count):
                moved = fast_dot(scaled[n], stack(around(now, n)[:, :width]))
                field[1 - now, n, :, pl.ds(0, width)] = solved_ref[n, :, here] + moved
            return carry

        lax.fori_loop(0, ITERS - 2, sweep, 0)
        for n in range(count):
            drive = source(n, units) + spread(n) * around(last, n)[:, :width]
            solved_ref[n, :, here] = fast_dot(plain[n], stack(drive))

    def solve_all(units, start):
        step = field.shape[-1] // LANES
        for i in range(0, len(units), step):
            solve(units[i:i + step], start + i * LANES)

    def product(j, start, width):
        out = None
        chunk = min(count, 8)
        for c in range(0, count, chunk):
            part = solved_ref[pl.ds(c, chunk), :, pl.ds(start, width)]
            top, low = halves(part.reshape(chunk * LANES, width))
            own = bits[j, pl.ds(c * LANES, chunk * LANES), :]
            part = fast_dot(own, top, TN) + fast_dot(own, low, TN)
            out = part if out is None else out + part
        return out

    def cast(j):
        for n in range(count):
            g, k = divmod(n, per)
            bits[j, pl.ds(n * LANES, LANES), :] = all_half[j, g, k].astype(BF16)

    @pl.when(leads)
    def _():
        own = [
            pltpu.make_async_copy(own_diagonal, all_diagonal.at[member], local.at[0]),
            pltpu.make_async_copy(own_link, all_link.at[member], local.at[1]),
            pltpu.make_async_copy(own_beside, all_beside.at[place], local.at[2]),
        ]
        for copy in own:
            copy.start()
        all_lines[member] = own_lines[...]
        all_inverse[member] = own_inverse[...]
        for j in range(2):
            all_half[j, member] = own_half[j]
        pl.semaphore_wait(barrier, members - 1)
        arrived(LINES, INVERSE)
        for n in range(count):
            g, k = divmod(n, per)
            weight_row = all_lines[g, per + k:per + k + 1, :]
            weight = as_columns(weight_row)
            inverse = all_inverse[g, k]
            weight_ref[n] = weight
            plain[n] = stacked(inverse)
            scaled[n] = stacked(weight * inverse * weight_row)
        for g in range(members):
            right_ref[:, pl.ds(g * share, share)] = all_lines[g, 2 * per:2 * per + 1, pl.ds(0, share)]
        arrived(FIRST)
        cast(0)
        solve_all(list(range(0, half, LANES)) + [None], 0)
        schur_ref[pl.ds(0, half), pl.ds(0, half + LANES)] = product(0, 0, half + LANES)
        arrived(SECOND)
        cast(1)
        solve_all(list(range(half, 2 * half, LANES)), half + LANES)
        schur_ref[pl.ds(0, half), pl.ds(half + LANES, half)] = product(0, half + LANES, half)
        schur_ref[pl.ds(half, half), pl.ds(half, half + LANES)] = product(1, half, half + LANES)
        arrived(DIAGONAL, LINK)
        for k, other in enumerate(others):
            @pl.when(lax.div(other, members // 2) == lax.div(lead, members // 2))
            def _():
                remote(BESIDE, other, k).wait_recv()
        for copy in own:
            copy.wait()


def solve_leaves(plan, arrays):
    coupling, _, _, _, _, _, parent_mat, _, link = arrays
    _, times, cells, rows, size = coupling.shape
    share, roots = link.shape[1:]
    per, members, half = times * cells, plan.members, size // 2
    count, wide = members * per, size + LANES
    SMEM = pl.BlockSpec(memory_space=pltpu.SMEM)
    lines = -(-(2 * per + 1) // 8) * 8
    shape = lambda *sizes: jax.ShapeDtypeStruct(sizes, F32)
    return pl.pallas_call(
        functools.partial(leaf_kernel, plan, neighbours(plan, times, cells), per),
        out_shape=[
            shape(size, wide),
            shape(count, rows, wide),
            shape(1, size),
            shape(members, share, half),
            shape(members // 2, share, half),
            shape(members, share, roots),
        ],
        in_specs=[VMEM, VMEM, VMEM, SMEM, VMEM, SMEM, VMEM, VMEM, VMEM],
        out_specs=[VMEM, VMEM, VMEM, ANY, ANY, ANY],
        scratch_shapes=[
            pltpu.VMEM((lines, LANES), F32),
            pltpu.VMEM((2, per, rows, half), F32),
            pltpu.VMEM((per, rows, rows), F32),
            pltpu.VMEM((share, half), F32),
            pltpu.VMEM((share, half), F32),
            pltpu.VMEM((share, roots), F32),
            pltpu.VMEM((members, lines, LANES), F32),
            pltpu.VMEM((2, members, per, rows, half), F32),
            pltpu.VMEM((members, per, rows, rows), F32),
            pltpu.VMEM((2, count, rows, half + LANES if count <= 8 else LANES), F32),
            pltpu.VMEM((count, rows, 3 * rows), BF16),
            pltpu.VMEM((count, rows, 3 * rows), BF16),
            pltpu.VMEM((count, rows, LANES), F32),
            pltpu.VMEM((2, count * rows, half), BF16),
            pltpu.SemaphoreType.DMA((7,)),
            pltpu.SemaphoreType.DMA((7, members - 1)),
            pltpu.SemaphoreType.DMA((3,)),
        ],
        compiler_params=pltpu.CompilerParams(
            collective_id=0, has_side_effects=True, vmem_limit_bytes=LIMIT
        ),
    )(*arrays)


def sum_kernel(plan, term_ref, total_ref, vector_ref, strips, vectors, whole,
               send, receive):
    scen, member = plan.here()
    lead = plan.leader(scen)
    count = plan.scen
    roots = whole.shape[0]
    rows = roots // count
    barrier = pltpu.get_barrier_semaphore()

    @pl.when(member == lead)
    def _():
        peers = [lax.rem(scen + k, count) for k in range(1, count)]
        devices = [plan.device(peer, plan.leader(peer)) for peer in peers]
        for device in devices:
            pl.semaphore_signal(barrier, inc=1, device_id=device, device_id_type=MESH)
        mine = pl.ds(pl.multiple_of(scen * rows, rows), rows)
        strips[scen] = term_ref[mine, :]
        vectors[scen] = term_ref[pl.ds(roots, 8), :]
        pl.semaphore_wait(barrier, count - 1)

        def remote(kind, k, source, target):
            return pltpu.make_async_remote_copy(
                src_ref=source, dst_ref=target, send_sem=send.at[kind, k],
                recv_sem=receive.at[kind, k], device_id=devices[k], device_id_type=MESH,
            )

        copies = []
        for k, peer in enumerate(peers):
            theirs = pl.ds(pl.multiple_of(peer * rows, rows), rows)
            copies.append(remote(0, k, term_ref.at[theirs, :], strips.at[scen]))
            copies.append(remote(1, k, term_ref.at[pl.ds(roots, 8), :], vectors.at[scen]))
        for copy in copies:
            copy.start()
        for copy in copies:
            copy.wait()
        total = strips[0]
        vector = vectors[0]
        for s in range(1, count):
            total = total + strips[s]
            vector = vector + vectors[s]
        vector_ref[...] = vector
        whole[mine, :] = total
        copies = [remote(2, k, whole.at[mine, :], whole.at[mine, :]) for k in range(count - 1)]
        for copy in copies:
            copy.start()
        for copy in copies:
            copy.wait()
        total_ref[...] = whole[...]

    @pl.when(member != lead)
    def _():
        total_ref[...] = jnp.zeros_like(total_ref)
        vector_ref[...] = jnp.zeros_like(vector_ref)


def sum_terms(plan, term):
    roots = term.shape[1]
    return pl.pallas_call(
        functools.partial(sum_kernel, plan),
        out_shape=[jax.ShapeDtypeStruct((roots, roots), F32), jax.ShapeDtypeStruct((8, roots), F32)],
        in_specs=[VMEM],
        out_specs=[VMEM] * 2,
        scratch_shapes=[
            pltpu.VMEM((plan.scen, roots // plan.scen, roots), F32),
            pltpu.VMEM((plan.scen, 8, roots), F32),
            pltpu.VMEM((roots, roots), F32),
            pltpu.SemaphoreType.DMA((3, plan.scen - 1)),
            pltpu.SemaphoreType.DMA((3, plan.scen - 1)),
        ],
        compiler_params=pltpu.CompilerParams(collective_id=1, has_side_effects=True),
    )(term)


def scatter_kernel(plan, pack_ref, leaf_ref, parent_ref, root_ref, landed, send, receive):
    times, cells = leaf_ref.shape[1:3]
    roots, share = root_ref.shape[0], parent_ref.shape[1]
    base = times * cells * LANES

    def write(line):
        for k in range(times * cells):
            t, c = divmod(k, cells)
            leaf_ref[0, t, c:c + 1, :] = line[:, k * LANES:(k + 1) * LANES]
        root_ref[...] = line[0, base:base + roots]
        parent_ref[...] = line[:, base + roots:base + roots + share]

    scen, member = plan.here()
    lead = plan.leader(scen)
    barrier = pltpu.get_barrier_semaphore()

    def remote(k, other):
        return pltpu.make_async_remote_copy(
            src_ref=pack_ref.at[other], dst_ref=landed, send_sem=send.at[k],
            recv_sem=receive, device_id=plan.device(scen, other), device_id_type=MESH,
        )

    @pl.when(member != lead)
    def _():
        pl.semaphore_signal(barrier, inc=1, device_id=plan.device(scen, lead), device_id_type=MESH)
        pl.semaphore_wait(barrier, 1)
        remote(0, lead).wait_recv()
        write(landed[0:1, :])

    @pl.when(member == lead)
    def _():
        others = [lax.rem(lead + k, plan.members) for k in range(1, plan.members)]
        for other in others:
            pl.semaphore_signal(
                barrier, inc=1, device_id=plan.device(scen, other), device_id_type=MESH
            )
        pl.semaphore_wait(barrier, plan.members - 1)
        copies = [remote(k, other) for k, other in enumerate(others)]
        for copy in copies:
            copy.start()
        write(pack_ref[member][0:1, :])
        for copy in copies:
            copy.wait_send()


def scatter(plan, pack, shapes):
    return pl.pallas_call(
        functools.partial(scatter_kernel, plan),
        out_shape=[jax.ShapeDtypeStruct(shape, F32) for shape in shapes],
        in_specs=[VMEM],
        out_specs=[VMEM] * 3,
        scratch_shapes=[
            pltpu.VMEM(pack.shape[1:], F32),
            pltpu.SemaphoreType.DMA((plan.members - 1,)),
            pltpu.SemaphoreType.DMA,
        ],
        compiler_params=pltpu.CompilerParams(collective_id=2, has_side_effects=True),
    )(pack)


def local_call(kernel, out_shape, count, scratch=()):
    many = isinstance(out_shape, list)
    return pl.pallas_call(
        kernel,
        out_shape=out_shape,
        in_specs=[VMEM] * count,
        out_specs=[VMEM] * len(out_shape) if many else VMEM,
        scratch_shapes=list(scratch),
        compiler_params=pltpu.CompilerParams(vmem_limit_bytes=LIMIT),
    )


def from_partner(block, axis, bit):
    count = lax.axis_size(axis)
    route = []
    for low in range(count):
        high = low | 1 << bit
        if high != low and high < count:
            route += [(low, high), (high, low)]
    return lax.ppermute(block, axis, route)


def neighbours(plan, times, cells):
    place = {}
    for g in range(plan.members):
        for t in range(times):
            for s in range(cells):
                at = ((g % plan.tm) * times + t, (g // plan.tm) * cells + s)
                place[at] = (g * times + t) * cells + s
    found = [None] * len(place)
    for (t, s), n in place.items():
        sides = [(t + 1, s), (t - 1, s), (t, s + 1), (t, s - 1)]
        found[n] = [place[side] for side in sides if side in place]
    return found


def body(
    plan,
    coupling,
    leaf_rhs,
    conductance,
    compressor,
    blocks,
    parent_of,
    parent_mat,
    parent_rhs,
    link,
    root_mat,
    root_rhs,
):
    _, times, cells, rows, size = coupling.shape
    per = times * cells
    roots = root_rhs.shape[0]
    share = parent_rhs.shape[1]
    schur, solved, right, diagonal, beside, all_link = solve_leaves(
        plan,
        [coupling, leaf_rhs, conductance, compressor, blocks, parent_of, parent_mat, parent_rhs, link],
    )
    for bit_index in range(plan.siblings.bit_length() - 1):
        schur = schur + from_partner(schur, "scen", bit_index)
    solution_p, term = local_call(
        functools.partial(parent_kernel, plan),
        [
            jax.ShapeDtypeStruct((size, roots + LANES), F32),
            jax.ShapeDtypeStruct((roots + 8, roots), F32),
        ],
        5,
    )(
        schur,
        diagonal.reshape(size, size // 2),
        beside.reshape(size // 2, size // 2),
        right,
        all_link.reshape(size, roots),
    )
    if plan.siblings > 1:
        term = jnp.where(lax.axis_index("scen") % plan.siblings == 0, term, 0.0)
    total, vector = sum_terms(plan, term)
    width = per * rows + roots + -(-share // LANES) * LANES
    pack = local_call(
        root_kernel, jax.ShapeDtypeStruct((plan.members, 8, width), F32), 6
    )(root_mat, total, vector, root_rhs[None], solution_p, solved)
    return scatter(plan, pack, [leaf_rhs.shape, (1, share), (roots,)])


def solution(mesh):
    return jax.shard_map(
        functools.partial(body, Plan(mesh)),
        mesh=mesh,
        in_specs=(
            P("scen", "tm", "space", None, None),
            P("scen", "tm", "space", None),
            P("scen", "tm", "space", None),
            P("scen", "tm", "space"),
            P("scen", "tm", "space", None, None),
            P("scen"),
            P(None, ("space", "tm"), None),
            P(None, ("space", "tm")),
            P(None, ("space", "tm"), None),
            P(),
            P(),
        ),
        out_specs=(P("scen", "tm", "space", None), P("scen", ("space", "tm")), P()),
        check_vma=False,
    )
```

```python
import functools

import jax
import jax.numpy as jnp
from jax import lax
from jax.experimental import pallas as pl
from jax.experimental.pallas import tpu as pltpu
from jax.sharding import PartitionSpec as P

PARENTS = 8
ITERS = 6
LANES = 128
F32 = jnp.float32
BF16 = jnp.bfloat16
HIGH = lax.Precision.HIGHEST
MESH = pl.DeviceIdType.MESH
VMEM = pl.BlockSpec(memory_space=pltpu.VMEM)
ANY = pl.BlockSpec(memory_space=pl.ANY)
LIMIT = 56 * 1024 * 1024
SETTLED = 3e-4
EXTRA = 16
NN = ((1,), (0,))
NT = ((1,), (1,))
TN = ((0,), (0,))


def full_dot(a, b, dims=NN):
    return lax.dot_general(a, b, (dims, ((), ())), precision=HIGH, preferred_element_type=F32)


def fast_dot(a, b, dims=NN):
    return lax.dot_general(a, b, (dims, ((), ())), preferred_element_type=F32)


def halves(x):
    top = x.astype(BF16)
    return top, (x - top.astype(F32)).astype(BF16)


def as_columns(row):
    return jnp.broadcast_to(row, (LANES, LANES)).T


def near_dot(a, b, dims=NN):
    a_top, a_low = halves(a)
    b_top, b_low = halves(b)
    return fast_dot(a_top, b_top, dims) + fast_dot(a_top, b_low, dims) + fast_dot(a_low, b_top, dims)


def spd_inverse(matrix, steps=None):
    size = matrix.shape[0]
    row = lax.broadcasted_iota(jnp.int32, (size, size), 0)
    column = lax.broadcasted_iota(jnp.int32, (size, size), 1)
    identity = jnp.where(row == column, 1.0, 0.0).astype(F32)
    square = near_dot(matrix, matrix)
    plain = jnp.max(jnp.sum(jnp.abs(matrix), axis=0, keepdims=True), axis=1, keepdims=True)
    squared = jnp.max(jnp.sum(jnp.abs(square), axis=0, keepdims=True), axis=1, keepdims=True)
    bound = jnp.maximum(jnp.minimum(plain, jnp.sqrt(squared)) * 1.0001, 1.0)
    total, spread = bound + 1.0, bound - 1.0
    scale = 1.0 / (2.0 * total * total - spread * spread)
    alpha, beta = 8.0 * total * scale, 8.0 * scale
    start = alpha * identity - beta * matrix
    residual = identity - alpha * matrix + beta * square

    def grow(x, r):
        both = near_dot(jnp.concatenate([x, r], axis=0), r)
        return x + both[:size], both[size:]

    def correct(_, x):
        return x + near_dot(x, identity - full_dot(matrix, x))

    if steps is not None:
        x, _ = lax.fori_loop(0, steps, lambda _, state: grow(*state), (start, residual))
        return lax.fori_loop(0, 2, correct, x)
    rho = jnp.max(spread * spread * scale)
    largest = jnp.max(bound)
    _, _, x, _ = lax.while_loop(
        lambda state: (state[0] > SETTLED) & (state[1] < 32),
        lambda state: (state[0] * state[0], state[1] + 1) + grow(*state[2:]),
        (rho, jnp.int32(0), start, residual),
    )
    rounds = 1 + (largest > 50.0).astype(jnp.int32) + (largest > 1000.0).astype(jnp.int32)
    return lax.fori_loop(0, rounds, correct, x)


def steps_for(bound):
    rho = (bound - 1.0) ** 2 / (2.0 * (bound + 1.0) ** 2 - (bound - 1.0) ** 2)
    steps = 0
    while rho > SETTLED:
        rho, steps = rho * rho, steps + 1
    return steps


def parent_kernel(plan, schur_ref, diagonal_ref, beside_ref, right_ref, link_ref, solution_ref, term_ref):
    half = diagonal_ref.shape[1]
    size = 2 * half
    roots = link_ref.shape[1]
    scen, _ = plan.here()
    near = lax.div(plan.leader(scen), plan.members // 2)
    reduced = schur_ref[pl.ds(half, 8), :][0:1] - right_ref[...]
    right = jnp.concatenate(
        [as_columns(reduced[:, c:c + LANES]) for c in range(0, size, LANES)], axis=0
    )
    a, b = pl.ds(0, half), pl.ds(half, half)
    behind = pl.ds(half + EXTRA, half)
    sides = jnp.concatenate([link_ref[...], right], axis=1)
    beside = beside_ref[...]
    h11 = diagonal_ref[a, :] + schur_ref[a, a]
    h21 = jnp.where(near == 0, beside.T, beside) + schur_ref[behind, a]
    h22 = diagonal_ref[b, :] + schur_ref[behind, b]
    x11 = spd_inverse(h11)
    across = full_dot(x11, h21, NT)
    ahead = full_dot(x11, sides[:half])
    x22 = spd_inverse(h22 - full_dot(h21, across))
    lower = near_dot(x22, sides[half:] - full_dot(h21, ahead))
    upper = ahead - near_dot(across, lower)
    solution_ref[a, :] = upper
    solution_ref[b, :] = lower
    term_ref[...] = near_dot(solution_ref[...], link_ref[...], TN)[:roots + 8]


def root_kernel(matrix_ref, term_ref, vector_ref, right_ref, solution_ref, solved_ref, pack_ref):
    roots = matrix_ref.shape[0]
    size = solution_ref.shape[0]
    groups = pack_ref.shape[0]
    half = size // 2
    width = solved_ref.shape[1] // groups
    share = size // groups
    inverse = spd_inverse(matrix_ref[...] + term_ref[...])
    root = full_dot(right_ref[...] - vector_ref[...], inverse)
    lane = lax.broadcasted_iota(jnp.int32, (8, LANES), 1)
    unit = jnp.where(lane == 0, 1.0, 0.0).astype(F32)
    parent = full_dot(jnp.concatenate([root, unit], axis=1), solution_ref[...], NT)
    leaf = (
        solved_ref[pl.ds(half, 8), :]
        - near_dot(parent[:, :half], solved_ref[pl.ds(0, half), :])
        - near_dot(parent[:, half:], solved_ref[pl.ds(half + EXTRA, half), :])
    )
    for g in range(groups):
        pack_ref[g, :, pl.ds(0, width)] = leaf[:, g * width:(g + 1) * width]
        pack_ref[g, :, pl.ds(width, roots)] = root
        pack_ref[g, :, pl.ds(width + roots, share)] = parent[:, g * share:(g + 1) * share]


def finish_kernel(line_ref, leaf_ref, parent_ref, root_ref):
    times, cells = leaf_ref.shape[1:3]
    roots, share = root_ref.shape[0], parent_ref.shape[1]
    base = times * cells * LANES
    for k in range(times * cells):
        t, c = divmod(k, cells)
        leaf_ref[0, t, c:c + 1, :] = line_ref[0:1, pl.ds(k * LANES, LANES)]
    root_ref[...] = line_ref[0, pl.ds(base, roots)]
    parent_ref[...] = line_ref[0:1, pl.ds(base + roots, share)]


class Plan:
    def __init__(self, mesh):
        self.scen, self.space, self.tm = (mesh.shape[name] for name in ("scen", "space", "tm"))
        self.members = self.space * self.tm
        self.siblings = self.scen // PARENTS

    def leader(self, scen):
        middle = self.members // 2
        if self.siblings == 1:
            return middle - lax.rem(scen, 2)
        return middle + 0 * scen

    def device(self, scen, member):
        return (scen, lax.div(member, self.tm), lax.rem(member, self.tm))

    def here(self):
        return lax.axis_index("scen"), lax.axis_index("space") * self.tm + lax.axis_index("tm")


def leaf_kernel(plan, beside, per, coupling_ref, rhs_ref, conductance_ref, compressor_ref, blocks_ref,
                parent_of_ref, parent_mat_ref, parent_rhs_ref, link_ref,
                schur_ref, solved_ref, right_ref, all_diagonal, all_beside, all_link,
                own_lines, own_half, own_inverse, own_diagonal, own_beside, own_link,
                all_lines, all_half, all_inverse,
                field, plain, scaled, bits, send, receive, local):
    count = len(beside)
    members = plan.members
    times, cells = coupling_ref.shape[1:3]
    half = coupling_ref.shape[-1] // 2
    share = parent_rhs_ref.shape[1]
    scen, member = plan.here()
    lead = plan.leader(scen)
    leads = member == lead
    close = lax.div(member, members // 2) == lax.div(lead, members // 2)
    place = lax.rem(member, members // 2)
    barrier = pltpu.get_barrier_semaphore()
    LINES, FIRST, INVERSE, SECOND, DIAGONAL, LINK, BESIDE = range(7)

    def remote(kind, at, slot):
        source, target = {
            LINES: (own_lines, all_lines.at[at]),
            FIRST: (own_half.at[0], all_half.at[0, at]),
            INVERSE: (own_inverse, all_inverse.at[at]),
            SECOND: (own_half.at[1], all_half.at[1, at]),
            DIAGONAL: (own_diagonal, all_diagonal.at[at]),
            LINK: (own_link, all_link.at[at]),
            BESIDE: (own_beside, all_beside.at[lax.rem(at, members // 2)]),
        }[kind]
        return pltpu.make_async_remote_copy(
            src_ref=source, dst_ref=target, send_sem=send.at[kind], recv_sem=receive.at[kind, slot],
            device_id=plan.device(scen, lead), device_id_type=MESH,
        )

    others = [lax.rem(lead + k, members) for k in range(1, members)]
    slot = lax.rem(member - lead + members, members) - 1

    @pl.when(leads)
    def _():
        for other in others:
            pl.semaphore_signal(
                barrier, inc=1, device_id=plan.device(scen, other), device_id_type=MESH
            )

    @pl.when(jnp.logical_not(leads))
    def _():
        pl.semaphore_signal(barrier, inc=1, device_id=plan.device(scen, lead), device_id_type=MESH)

    label = parent_of_ref[0]
    own_lines[...] = jnp.zeros_like(own_lines)
    for k in range(per):
        t, c = divmod(k, cells)
        own_lines[k:k + 1, :] = rhs_ref[0, t, c:c + 1, :]
        doubled = 1.0 + compressor_ref[0, t, c].astype(F32)
        own_lines[per + k:per + k + 1, :] = conductance_ref[0, t, c:c + 1, :] * doubled * 0.5
        for j in range(2):
            own_half[j, k] = coupling_ref[0, t, c, :, pl.ds(j * half, half)].astype(F32).T
    own_lines[2 * per:2 * per + 1, pl.ds(0, share)] = parent_rhs_ref[pl.ds(label, 1), :]

    @pl.when(jnp.logical_not(leads))
    def _():
        pl.semaphore_wait(barrier, 1)
        remote(LINES, member, slot).start()
        remote(FIRST, member, slot).start()

    rows = blocks_ref.shape[-1]
    zero = jnp.zeros((rows, rows), F32)
    for i in range(0, per, 2):
        j = min(i + 1, per - 1)
        first = blocks_ref[0, i // cells, i % cells]
        second = blocks_ref[0, j // cells, j % cells]
        pair = jnp.concatenate(
            [jnp.concatenate([first, zero], axis=1), jnp.concatenate([zero, second], axis=1)], axis=0
        )
        found = spd_inverse(pair, steps_for(8.0 * rows))
        own_inverse[i] = found[:rows, :rows]
        own_inverse[j] = found[rows:, rows:]
    strip = parent_mat_ref[label]
    lower = lax.div(member, members // 2) == 0
    own_diagonal[...] = jnp.where(lower, strip[:, :half], strip[:, half:])
    own_beside[...] = jnp.where(lower, strip[:, half:], strip[:, :half])
    own_link[...] = link_ref[label]

    @pl.when(jnp.logical_not(leads))
    def _():
        remote(INVERSE, member, slot).start()
        remote(SECOND, member, slot).start()
        for kind in (LINES, FIRST, INVERSE, SECOND):
            remote(kind, member, slot).wait_send()
        remote(DIAGONAL, member, slot).start()
        remote(LINK, member, slot).start()

        @pl.when(close)
        def _():
            remote(BESIDE, member, slot).start()
            remote(BESIDE, member, slot).wait_send()

        remote(DIAGONAL, member, slot).wait_send()
        remote(LINK, member, slot).wait_send()

    def arrived(*kinds):
        for kind in kinds:
            for k, other in enumerate(others):
                remote(kind, other, k).wait_recv()

    def tile(matrix):
        top, low = halves(matrix)
        return jnp.concatenate(
            [
                jnp.concatenate([top, low], axis=1),
                jnp.concatenate([top, jnp.zeros_like(top)], axis=1),
            ],
            axis=0,
        )

    def apply(x, matrix):
        both = fast_dot(jnp.concatenate(halves(x), axis=1), matrix)
        return both[:, :LANES] + both[:, LANES:]

    def source(j, n):
        g, k = divmod(n, per)
        if j == 1:
            return all_half[j, g, k]
        right = jnp.broadcast_to(all_lines[g, k:k + 1, :], (EXTRA, LANES))
        return jnp.concatenate([all_half[j, g, k], right], axis=0)

    def weight(n):
        g, k = divmod(n, per)
        return all_lines[g, per + k:per + k + 1, :]

    def lanes(n):
        return pl.ds(n * LANES, LANES)

    def around(at, n, width):
        total = field[at, pl.ds(0, width), lanes(beside[n][0])]
        for m in beside[n][1:]:
            total = total + field[at, pl.ds(0, width), lanes(m)]
        return total

    last = (ITERS - 2) % 2

    def solve(j):
        start, width = (half + EXTRA, half) if j else (0, half + EXTRA)
        here, top = pl.ds(start, width), pl.ds(0, width)
        for n in range(count):
            g, k = divmod(n, per)
            bits[j, :, lanes(n)] = all_half[j, g, k].astype(BF16)
            first = weight(n) * apply(source(j, n), plain[n])
            field[0, top, lanes(n)] = first
            solved_ref[here, lanes(n)] = first

        def sweep(k, carry):
            now = lax.rem(k, 2)
            for n in range(count):
                moved = apply(around(now, n, width), scaled[n])
                field[1 - now, top, lanes(n)] = solved_ref[here, lanes(n)] + moved
            return carry

        lax.fori_loop(0, ITERS - 2, sweep, 0)
        for n in range(count):
            drive = source(j, n) + weight(n) * around(last, n, width)
            solved_ref[here, lanes(n)] = apply(drive, plain[n])

    def product(start, width, j):
        top, low = halves(solved_ref[pl.ds(start, width), :])
        schur_ref[pl.ds(start, width), pl.ds(j * half, half)] = (
            fast_dot(top, bits[j], NT) + fast_dot(low, bits[j], NT)
        )

    @pl.when(leads)
    def _():
        own = [
            pltpu.make_async_copy(own_diagonal, all_diagonal.at[member], local.at[0]),
            pltpu.make_async_copy(own_link, all_link.at[member], local.at[1]),
            pltpu.make_async_copy(own_beside, all_beside.at[place], local.at[2]),
        ]
        for copy in own:
            copy.start()
        all_lines[member] = own_lines[...]
        all_inverse[member] = own_inverse[...]
        for j in range(2):
            all_half[j, member] = own_half[j]
        pl.semaphore_wait(barrier, members - 1)
        arrived(LINES, INVERSE)
        for n in range(count):
            g, k = divmod(n, per)
            inverse = all_inverse[g, k]
            plain[n] = tile(inverse)
            scaled[n] = tile(as_columns(weight(n)) * inverse * weight(n))
        for g in range(members):
            right_ref[:, pl.ds(g * share, share)] = all_lines[g, 2 * per:2 * per + 1, pl.ds(0, share)]
        arrived(FIRST)
        solve(0)
        product(0, half + EXTRA, 0)
        arrived(SECOND)
        solve(1)
        product(half + EXTRA, half, 0)
        product(half, half + EXTRA, 1)
        arrived(DIAGONAL, LINK)
        for k, other in enumerate(others):
            @pl.when(lax.div(other, members // 2) == lax.div(lead, members // 2))
            def _():
                remote(BESIDE, other, k).wait_recv()
        for copy in own:
            copy.wait()


def solve_leaves(plan, arrays):
    coupling, _, _, _, _, _, parent_mat, _, link = arrays
    _, times, cells, rows, size = coupling.shape
    share, roots = link.shape[1:]
    per, members, half = times * cells, plan.members, size // 2
    count, wide = members * per, size + EXTRA
    SMEM = pl.BlockSpec(memory_space=pltpu.SMEM)
    lines = -(-(2 * per + 1) // 8) * 8
    shape = lambda *sizes: jax.ShapeDtypeStruct(sizes, F32)
    return pl.pallas_call(
        functools.partial(leaf_kernel, plan, neighbours(plan, times, cells), per),
        out_shape=[
            shape(wide, size),
            shape(wide, count * rows),
            shape(1, size),
            shape(members, share, half),
            shape(members // 2, share, half),
            shape(members, share, roots),
        ],
        in_specs=[VMEM, VMEM, VMEM, SMEM, VMEM, SMEM, VMEM, VMEM, VMEM],
        out_specs=[VMEM, VMEM, VMEM, ANY, ANY, ANY],
        scratch_shapes=[
            pltpu.VMEM((lines, LANES), F32),
            pltpu.VMEM((2, per, half, rows), F32),
            pltpu.VMEM((per, rows, rows), F32),
            pltpu.VMEM((share, half), F32),
            pltpu.VMEM((share, half), F32),
            pltpu.VMEM((share, roots), F32),
            pltpu.VMEM((members, lines, LANES), F32),
            pltpu.VMEM((2, members, per, half, rows), F32),
            pltpu.VMEM((members, per, rows, rows), F32),
            pltpu.VMEM((2, half + EXTRA, count * rows), F32),
            pltpu.VMEM((count, 2 * rows, 2 * rows), BF16),
            pltpu.VMEM((count, 2 * rows, 2 * rows), BF16),
            pltpu.VMEM((2, half, count * rows), BF16),
            pltpu.SemaphoreType.DMA((7,)),
            pltpu.SemaphoreType.DMA((7, members - 1)),
            pltpu.SemaphoreType.DMA((3,)),
        ],
        compiler_params=pltpu.CompilerParams(
            collective_id=0, has_side_effects=True, vmem_limit_bytes=LIMIT
        ),
    )(*arrays)


def sum_kernel(plan, term_ref, total_ref, vector_ref, strips, vectors, whole,
               send, receive):
    scen, member = plan.here()
    lead = plan.leader(scen)
    count = plan.scen
    roots = whole.shape[0]
    rows = roots // count
    barrier = pltpu.get_barrier_semaphore()

    @pl.when(member == lead)
    def _():
        peers = [lax.rem(scen + k, count) for k in range(1, count)]
        devices = [plan.device(peer, plan.leader(peer)) for peer in peers]
        for device in devices:
            pl.semaphore_signal(barrier, inc=1, device_id=device, device_id_type=MESH)
        mine = pl.ds(pl.multiple_of(scen * rows, rows), rows)
        strips[scen] = term_ref[mine, :]
        vectors[scen] = term_ref[pl.ds(roots, 8), :]
        pl.semaphore_wait(barrier, count - 1)

        def remote(kind, k, source, target):
            return pltpu.make_async_remote_copy(
                src_ref=source, dst_ref=target, send_sem=send.at[kind, k],
                recv_sem=receive.at[kind, k], device_id=devices[k], device_id_type=MESH,
            )

        copies = []
        for k, peer in enumerate(peers):
            theirs = pl.ds(pl.multiple_of(peer * rows, rows), rows)
            copies.append(remote(0, k, term_ref.at[theirs, :], strips.at[scen]))
            copies.append(remote(1, k, term_ref.at[pl.ds(roots, 8), :], vectors.at[scen]))
        for copy in copies:
            copy.start()
        for copy in copies:
            copy.wait()
        total = strips[0]
        vector = vectors[0]
        for s in range(1, count):
            total = total + strips[s]
            vector = vector + vectors[s]
        vector_ref[...] = vector
        whole[mine, :] = total
        copies = [remote(2, k, whole.at[mine, :], whole.at[mine, :]) for k in range(count - 1)]
        for copy in copies:
            copy.start()
        for copy in copies:
            copy.wait()
        total_ref[...] = whole[...]

    @pl.when(member != lead)
    def _():
        total_ref[...] = jnp.zeros_like(total_ref)
        vector_ref[...] = jnp.zeros_like(vector_ref)


def sum_terms(plan, term):
    roots = term.shape[1]
    return pl.pallas_call(
        functools.partial(sum_kernel, plan),
        out_shape=[jax.ShapeDtypeStruct((roots, roots), F32), jax.ShapeDtypeStruct((8, roots), F32)],
        in_specs=[VMEM],
        out_specs=[VMEM] * 2,
        scratch_shapes=[
            pltpu.VMEM((plan.scen, roots // plan.scen, roots), F32),
            pltpu.VMEM((plan.scen, 8, roots), F32),
            pltpu.VMEM((roots, roots), F32),
            pltpu.SemaphoreType.DMA((3, plan.scen - 1)),
            pltpu.SemaphoreType.DMA((3, plan.scen - 1)),
        ],
        compiler_params=pltpu.CompilerParams(collective_id=1, has_side_effects=True),
    )(term)


def scatter_kernel(plan, pack_ref, out_ref, landed, send, receive):
    scen, member = plan.here()
    lead = plan.leader(scen)
    barrier = pltpu.get_barrier_semaphore()

    def remote(k, other):
        return pltpu.make_async_remote_copy(
            src_ref=pack_ref.at[other], dst_ref=landed, send_sem=send.at[k],
            recv_sem=receive, device_id=plan.device(scen, other), device_id_type=MESH,
        )

    @pl.when(member != lead)
    def _():
        pl.semaphore_signal(barrier, inc=1, device_id=plan.device(scen, lead), device_id_type=MESH)
        pl.semaphore_wait(barrier, 1)
        remote(0, lead).wait_recv()
        out_ref[...] = landed[...]

    @pl.when(member == lead)
    def _():
        others = [lax.rem(lead + k, plan.members) for k in range(1, plan.members)]
        for other in others:
            pl.semaphore_signal(
                barrier, inc=1, device_id=plan.device(scen, other), device_id_type=MESH
            )
        pl.semaphore_wait(barrier, plan.members - 1)
        copies = [remote(k, other) for k, other in enumerate(others)]
        for copy in copies:
            copy.start()
        out_ref[...] = pack_ref[member]
        for copy in copies:
            copy.wait_send()


def scatter(plan, pack):
    return pl.pallas_call(
        functools.partial(scatter_kernel, plan),
        out_shape=jax.ShapeDtypeStruct(pack.shape[1:], F32),
        in_specs=[VMEM],
        out_specs=VMEM,
        scratch_shapes=[
            pltpu.VMEM(pack.shape[1:], F32),
            pltpu.SemaphoreType.DMA((plan.members - 1,)),
            pltpu.SemaphoreType.DMA,
        ],
        compiler_params=pltpu.CompilerParams(collective_id=2, has_side_effects=True),
    )(pack)


def local_call(kernel, out_shape, count, scratch=()):
    many = isinstance(out_shape, list)
    return pl.pallas_call(
        kernel,
        out_shape=out_shape,
        in_specs=[VMEM] * count,
        out_specs=[VMEM] * len(out_shape) if many else VMEM,
        scratch_shapes=list(scratch),
        compiler_params=pltpu.CompilerParams(vmem_limit_bytes=LIMIT),
    )


def from_partner(block, axis, bit):
    count = lax.axis_size(axis)
    route = []
    for low in range(count):
        high = low | 1 << bit
        if high != low and high < count:
            route += [(low, high), (high, low)]
    return lax.ppermute(block, axis, route)


def neighbours(plan, times, cells):
    place = {}
    for g in range(plan.members):
        for t in range(times):
            for s in range(cells):
                at = ((g % plan.tm) * times + t, (g // plan.tm) * cells + s)
                place[at] = (g * times + t) * cells + s
    found = [None] * len(place)
    for (t, s), n in place.items():
        sides = [(t + 1, s), (t - 1, s), (t, s + 1), (t, s - 1)]
        found[n] = [place[side] for side in sides if side in place]
    return found


def body(
    plan,
    coupling,
    leaf_rhs,
    conductance,
    compressor,
    blocks,
    parent_of,
    parent_mat,
    parent_rhs,
    link,
    root_mat,
    root_rhs,
):
    _, times, cells, rows, size = coupling.shape
    per = times * cells
    roots = root_rhs.shape[0]
    share = parent_rhs.shape[1]
    schur, solved, right, diagonal, beside, all_link = solve_leaves(
        plan,
        [coupling, leaf_rhs, conductance, compressor, blocks, parent_of, parent_mat, parent_rhs, link],
    )
    for bit_index in range(plan.siblings.bit_length() - 1):
        schur = schur + from_partner(schur, "scen", bit_index)
    solution_p, term = local_call(
        functools.partial(parent_kernel, plan),
        [
            jax.ShapeDtypeStruct((size, roots + LANES), F32),
            jax.ShapeDtypeStruct((roots + 8, roots), F32),
        ],
        5,
    )(
        schur,
        diagonal.reshape(size, size // 2),
        beside.reshape(size // 2, size // 2),
        right,
        all_link.reshape(size, roots),
    )
    if plan.siblings > 1:
        term = jnp.where(lax.axis_index("scen") % plan.siblings == 0, term, 0.0)
    total, vector = sum_terms(plan, term)
    width = per * rows + roots + -(-share // LANES) * LANES
    pack = local_call(
        root_kernel, jax.ShapeDtypeStruct((plan.members, 8, width), F32), 6
    )(root_mat, total, vector, root_rhs[None], solution_p, solved)
    shapes = [leaf_rhs.shape, (1, share), (roots,)]
    return tuple(
        local_call(finish_kernel, [jax.ShapeDtypeStruct(shape, F32) for shape in shapes], 1)(
            scatter(plan, pack)
        )
    )


def solution(mesh):
    return jax.shard_map(
        functools.partial(body, Plan(mesh)),
        mesh=mesh,
        in_specs=(
            P("scen", "tm", "space", None, None),
            P("scen", "tm", "space", None),
            P("scen", "tm", "space", None),
            P("scen", "tm", "space"),
            P("scen", "tm", "space", None, None),
            P("scen"),
            P(None, ("space", "tm"), None),
            P(None, ("space", "tm")),
            P(None, ("space", "tm"), None),
            P(),
            P(),
        ),
        out_specs=(P("scen", "tm", "space", None), P("scen", ("space", "tm")), P()),
        check_vma=False,
    )
```

```python
import functools

import jax
import jax.numpy as jnp
from jax import lax
from jax.experimental import pallas as pl
from jax.experimental.pallas import tpu as pltpu
from jax.sharding import PartitionSpec as P

PARENTS = 8
ITERS = 6
LANES = 128
F32 = jnp.float32
BF16 = jnp.bfloat16
HIGH = lax.Precision.HIGHEST
MESH = pl.DeviceIdType.MESH
VMEM = pl.BlockSpec(memory_space=pltpu.VMEM)
ANY = pl.BlockSpec(memory_space=pl.ANY)
LIMIT = 56 * 1024 * 1024
SETTLED = 3e-4
EXTRA = 16
NN = ((1,), (0,))
NT = ((1,), (1,))
TN = ((0,), (0,))


def full_dot(a, b, dims=NN):
    return lax.dot_general(a, b, (dims, ((), ())), precision=HIGH, preferred_element_type=F32)


def fast_dot(a, b, dims=NN):
    return lax.dot_general(a, b, (dims, ((), ())), preferred_element_type=F32)


def halves(x):
    top = x.astype(BF16)
    return top, (x - top.astype(F32)).astype(BF16)


def as_columns(row):
    return jnp.broadcast_to(row, (LANES, LANES)).T


def near_dot(a, b, dims=NN):
    a_top, a_low = halves(a)
    b_top, b_low = halves(b)
    return fast_dot(a_top, b_top, dims) + fast_dot(a_top, b_low, dims) + fast_dot(a_low, b_top, dims)


def spd_inverse(matrix, steps=None):
    size = matrix.shape[0]
    row = lax.broadcasted_iota(jnp.int32, (size, size), 0)
    column = lax.broadcasted_iota(jnp.int32, (size, size), 1)
    identity = jnp.where(row == column, 1.0, 0.0).astype(F32)
    square = near_dot(matrix, matrix)
    plain = jnp.max(jnp.sum(jnp.abs(matrix), axis=0, keepdims=True), axis=1, keepdims=True)
    squared = jnp.max(jnp.sum(jnp.abs(square), axis=0, keepdims=True), axis=1, keepdims=True)
    bound = jnp.maximum(jnp.minimum(plain, jnp.sqrt(squared)) * 1.0001, 1.0)
    total, spread = bound + 1.0, bound - 1.0
    scale = 1.0 / (2.0 * total * total - spread * spread)
    alpha, beta = 8.0 * total * scale, 8.0 * scale
    start = alpha * identity - beta * matrix
    residual = identity - alpha * matrix + beta * square

    def grow(x, r):
        both = near_dot(jnp.concatenate([x, r], axis=0), r)
        return x + both[:size], both[size:]

    def correct(_, x):
        left = identity - full_dot(matrix, x)
        return x + fast_dot(x.astype(BF16), left.astype(BF16))

    if steps is not None:
        x, _ = lax.fori_loop(0, steps, lambda _, state: grow(*state), (start, residual))
        return lax.fori_loop(0, 2, correct, x)
    rho = jnp.max(spread * spread * scale)
    largest = jnp.max(bound)
    _, _, x, _ = lax.while_loop(
        lambda state: (state[0] > SETTLED) & (state[1] < 32),
        lambda state: (state[0] * state[0], state[1] + 1) + grow(*state[2:]),
        (rho, jnp.int32(0), start, residual),
    )
    rounds = 1 + (largest > 50.0).astype(jnp.int32) + (largest > 1000.0).astype(jnp.int32)
    return lax.fori_loop(0, rounds, correct, x)


def steps_for(bound):
    rho = (bound - 1.0) ** 2 / (2.0 * (bound + 1.0) ** 2 - (bound - 1.0) ** 2)
    steps = 0
    while rho > SETTLED:
        rho, steps = rho * rho, steps + 1
    return steps


def parent_kernel(plan, schur_ref, corner_ref, diagonal_ref, beside_ref, right_ref, link_ref,
                  solution_ref, term_ref):
    part = diagonal_ref.shape[1]
    half = 2 * part
    size = 2 * half
    roots = link_ref.shape[1]
    scen, _ = plan.here()
    near = lax.div(plan.leader(scen), plan.members // 2)
    reduced = schur_ref[pl.ds(half, 8), :][0:1] - right_ref[...]
    right = jnp.concatenate(
        [as_columns(reduced[:, c:c + LANES]) for c in range(0, size, LANES)], axis=0
    )
    a, b = pl.ds(0, half), pl.ds(half, half)
    behind = pl.ds(half + EXTRA, half)
    sides = jnp.concatenate([link_ref[...], right], axis=1)
    beside = beside_ref[...]

    def diagonal(start):
        upper = jnp.concatenate(
            [corner_ref[pl.ds(start, part), :], diagonal_ref[pl.ds(start, part), :]], axis=1
        )
        lower = jnp.concatenate(
            [upper[:, part:].T, diagonal_ref[pl.ds(start + part, part), :]], axis=1
        )
        return jnp.concatenate([upper, lower], axis=0)

    h11 = diagonal(0) + schur_ref[a, a]
    h21 = jnp.where(near == 0, beside.T, beside) + schur_ref[behind, a]
    h22 = diagonal(half) + schur_ref[behind, b]
    x11 = spd_inverse(h11)
    across = full_dot(x11, h21, NT)
    ahead = near_dot(x11, sides[:half])
    x22 = spd_inverse(h22 - full_dot(h21, across))
    lower = near_dot(x22, sides[half:] - near_dot(h21, ahead))
    upper = ahead - near_dot(across, lower)
    solution_ref[a, :] = upper
    solution_ref[b, :] = lower
    term_ref[...] = near_dot(solution_ref[...], link_ref[...], TN)[:roots + 8]


def root_kernel(matrix_ref, term_ref, vector_ref, right_ref, solution_any, solved_any, pack_ref,
                solution_ref, solved_ref, local):
    loads = [
        pltpu.make_async_copy(solution_any, solution_ref, local.at[0]),
        pltpu.make_async_copy(solved_any, solved_ref, local.at[1]),
    ]
    for load in loads:
        load.start()
    roots = matrix_ref.shape[0]
    size = solution_ref.shape[0]
    groups = pack_ref.shape[0]
    half = size // 2
    width = solved_ref.shape[1] // groups
    share = size // groups
    inverse = spd_inverse(matrix_ref[...] + term_ref[...])
    root = full_dot(right_ref[...] - vector_ref[...], inverse)
    for load in loads:
        load.wait()
    lane = lax.broadcasted_iota(jnp.int32, (8, LANES), 1)
    unit = jnp.where(lane == 0, 1.0, 0.0).astype(F32)
    parent = full_dot(jnp.concatenate([root, unit], axis=1), solution_ref[...], NT)
    leaf = (
        solved_ref[pl.ds(half, 8), :]
        - near_dot(parent[:, :half], solved_ref[pl.ds(0, half), :])
        - near_dot(parent[:, half:], solved_ref[pl.ds(half + EXTRA, half), :])
    )
    for g in range(groups):
        pack_ref[g, :, pl.ds(0, width)] = leaf[:, g * width:(g + 1) * width]
        pack_ref[g, :, pl.ds(width, roots)] = root
        pack_ref[g, :, pl.ds(width + roots, share)] = parent[:, g * share:(g + 1) * share]


def finish_kernel(line_ref, leaf_ref, parent_ref, root_ref):
    times, cells = leaf_ref.shape[1:3]
    roots, share = root_ref.shape[0], parent_ref.shape[1]
    base = times * cells * LANES
    for k in range(times * cells):
        t, c = divmod(k, cells)
        leaf_ref[0, t, c:c + 1, :] = line_ref[0:1, pl.ds(k * LANES, LANES)]
    root_ref[...] = line_ref[0, pl.ds(base, roots)]
    parent_ref[...] = line_ref[0:1, pl.ds(base + roots, share)]


class Plan:
    def __init__(self, mesh):
        self.scen, self.space, self.tm = (mesh.shape[name] for name in ("scen", "space", "tm"))
        self.members = self.space * self.tm
        self.siblings = self.scen // PARENTS

    def leader(self, scen):
        middle = self.members // 2
        if self.siblings == 1:
            return middle - lax.rem(scen, 2)
        return middle + 0 * scen

    def device(self, scen, member):
        return (scen, lax.div(member, self.tm), lax.rem(member, self.tm))

    def here(self):
        return lax.axis_index("scen"), lax.axis_index("space") * self.tm + lax.axis_index("tm")


def leaf_kernel(plan, beside, per, coupling_ref, rhs_ref, conductance_ref, compressor_ref, blocks_ref,
                parent_of_ref, parent_mat_ref, parent_rhs_ref, link_ref,
                schur_ref, solved_ref, right_ref, all_corner, all_diagonal, all_beside, all_link,
                own_lines, own_half, own_inverse, own_corner, own_diagonal, own_beside, own_link,
                mats, links, own_diag, all_diag,
                all_lines, all_half, all_inverse,
                field, plain, scaled, bits, send, receive, local):
    count = len(beside)
    members = plan.members
    packed = per % 2 == 0
    times, cells = coupling_ref.shape[1:3]
    half = coupling_ref.shape[-1] // 2
    share = parent_rhs_ref.shape[1]
    scen, member = plan.here()
    lead = plan.leader(scen)
    leads = member == lead
    close = lax.div(member, members // 2) == lax.div(lead, members // 2)
    place = lax.rem(member, members // 2)
    barrier = pltpu.get_barrier_semaphore()
    LINES, FIRST, INVERSE, SECOND, DIAGONAL, LINK, BESIDE, CORNER, DIAG = range(9)
    part = half // 2
    cornered = place * share < part
    loads = [
        pltpu.make_async_copy(parent_mat_ref, mats, local.at[4]),
        pltpu.make_async_copy(link_ref, links, local.at[5]),
    ]
    for load in loads:
        load.start()

    def remote(kind, at, slot):
        source, target = {
            LINES: (own_lines, all_lines.at[at]),
            FIRST: (own_half.at[0], all_half.at[0, at]),
            INVERSE: (own_inverse, all_inverse.at[at]),
            SECOND: (own_half.at[1], all_half.at[1, at]),
            DIAGONAL: (own_diagonal, all_diagonal.at[at]),
            CORNER: (own_corner, all_corner.at[at]),
            DIAG: (own_diag, all_diag.at[at]),
            LINK: (own_link, all_link.at[at]),
            BESIDE: (own_beside, all_beside.at[lax.rem(at, members // 2)]),
        }[kind]
        return pltpu.make_async_remote_copy(
            src_ref=source, dst_ref=target, send_sem=send.at[kind], recv_sem=receive.at[kind, slot],
            device_id=plan.device(scen, lead), device_id_type=MESH,
        )

    others = [lax.rem(lead + k, members) for k in range(1, members)]
    slot = lax.rem(member - lead + members, members) - 1

    @pl.when(leads)
    def _():
        for other in others:
            pl.semaphore_signal(
                barrier, inc=1, device_id=plan.device(scen, other), device_id_type=MESH
            )

    @pl.when(jnp.logical_not(leads))
    def _():
        pl.semaphore_signal(barrier, inc=1, device_id=plan.device(scen, lead), device_id_type=MESH)

    label = parent_of_ref[0]
    own_lines[...] = jnp.zeros_like(own_lines)
    own_diag[...] = jnp.zeros_like(own_diag)
    for k in range(per):
        t, c = divmod(k, cells)
        own_lines[k:k + 1, :] = rhs_ref[0, t, c:c + 1, :]
        doubled = 1.0 + compressor_ref[0, t, c].astype(F32)
        own_lines[per + k:per + k + 1, :] = conductance_ref[0, t, c:c + 1, :] * doubled * 0.5
        for j in range(2):
            own_half[j, k] = coupling_ref[0, t, c, :, pl.ds(j * half, half)].astype(F32).T
    own_lines[2 * per:2 * per + 1, pl.ds(0, share)] = parent_rhs_ref[pl.ds(label, 1), :]

    @pl.when(jnp.logical_not(leads))
    def _():
        pl.semaphore_wait(barrier, 1)
        remote(LINES, member, slot).start()
        remote(FIRST, member, slot).start()

    rows = blocks_ref.shape[-1]
    zero = jnp.zeros((rows, rows), F32)
    for i in range(0, per, 2):
        j = min(i + 1, per - 1)
        first = blocks_ref[0, i // cells, i % cells]
        second = blocks_ref[0, j // cells, j % cells]
        pair = jnp.concatenate(
            [jnp.concatenate([first, zero], axis=1), jnp.concatenate([zero, second], axis=1)], axis=0
        )
        found = spd_inverse(pair, steps_for(8.0 * rows))
        if packed:
            row = lax.broadcasted_iota(jnp.int32, (rows, rows), 0)
            column = lax.broadcasted_iota(jnp.int32, (rows, rows), 1)
            own_inverse[i // 2] = jnp.where(row <= column, found[:rows, :rows], found[rows:, rows:])
            kept = jnp.where(row == column, found[rows:, rows:], 0.0)
            own_diag[i // 2:i // 2 + 1, :] = jnp.sum(kept, axis=0, keepdims=True)
        else:
            own_inverse[i] = found[:rows, :rows]
            own_inverse[j] = found[rows:, rows:]
    for load in loads:
        load.wait()
    strip = mats[label]
    lower = lax.div(member, members // 2) == 0
    square = jnp.where(lower, strip[:, :half], strip[:, half:])
    own_corner[...] = square[:, :part]
    own_diagonal[...] = square[:, part:]
    own_beside[...] = jnp.where(lower, strip[:, half:], strip[:, :half])
    own_link[...] = links[label]

    @pl.when(jnp.logical_not(leads))
    def _():
        remote(INVERSE, member, slot).start()
        remote(DIAG, member, slot).start()
        remote(SECOND, member, slot).start()
        for kind in (LINES, FIRST, INVERSE, DIAG, SECOND):
            remote(kind, member, slot).wait_send()
        remote(DIAGONAL, member, slot).start()
        remote(LINK, member, slot).start()

        @pl.when(cornered)
        def _():
            remote(CORNER, member, slot).start()
            remote(CORNER, member, slot).wait_send()

        @pl.when(close)
        def _():
            remote(BESIDE, member, slot).start()
            remote(BESIDE, member, slot).wait_send()

        remote(DIAGONAL, member, slot).wait_send()
        remote(LINK, member, slot).wait_send()

    def arrived(*kinds):
        for kind in kinds:
            for k, other in enumerate(others):
                remote(kind, other, k).wait_recv()

    def unpacked(g, k):
        if not packed:
            return all_inverse[g, k]
        both = all_inverse[g, k // 2]
        other = both.T
        row = lax.broadcasted_iota(jnp.int32, both.shape, 0)
        column = lax.broadcasted_iota(jnp.int32, both.shape, 1)
        if k % 2 == 0:
            return jnp.where(row <= column, both, other)
        middle = jnp.broadcast_to(all_diag[g, k // 2:k // 2 + 1, :], both.shape)
        return jnp.where(row > column, both, jnp.where(row < column, other, middle))

    def tile(matrix):
        top, low = halves(matrix)
        return jnp.concatenate(
            [
                jnp.concatenate([top, low], axis=1),
                jnp.concatenate([top, jnp.zeros_like(top)], axis=1),
            ],
            axis=0,
        )

    def apply(x, matrix):
        both = fast_dot(jnp.concatenate(halves(x), axis=1), matrix)
        return both[:, :LANES] + both[:, LANES:]

    def source(j, n):
        g, k = divmod(n, per)
        if j == 1:
            return all_half[j, g, k]
        right = jnp.broadcast_to(all_lines[g, k:k + 1, :], (EXTRA, LANES))
        return jnp.concatenate([all_half[j, g, k], right], axis=0)

    def weight(n):
        g, k = divmod(n, per)
        return all_lines[g, per + k:per + k + 1, :]

    def lanes(n):
        return pl.ds(n * LANES, LANES)

    def around(at, n, width):
        total = field[at, pl.ds(0, width), lanes(beside[n][0])]
        for m in beside[n][1:]:
            total = total + field[at, pl.ds(0, width), lanes(m)]
        return total

    last = (ITERS - 2) % 2

    def solve(j):
        start, width = (half + EXTRA, half) if j else (0, half + EXTRA)
        here, top = pl.ds(start, width), pl.ds(0, width)
        for n in range(count):
            g, k = divmod(n, per)
            bits[j, :, lanes(n)] = all_half[j, g, k].astype(BF16)
            first = weight(n) * apply(source(j, n), plain[n])
            field[0, top, lanes(n)] = first
            solved_ref[here, lanes(n)] = first

        def sweep(k, carry):
            now = lax.rem(k, 2)
            for n in range(count):
                moved = apply(around(now, n, width), scaled[n])
                field[1 - now, top, lanes(n)] = solved_ref[here, lanes(n)] + moved
            return carry

        lax.fori_loop(0, ITERS - 2, sweep, 0)
        for n in range(count):
            drive = source(j, n) + weight(n) * around(last, n, width)
            solved_ref[here, lanes(n)] = apply(drive, plain[n])

    def product(start, width, j):
        top, low = halves(solved_ref[pl.ds(start, width), :])
        schur_ref[pl.ds(start, width), pl.ds(j * half, half)] = (
            fast_dot(top, bits[j], NT) + fast_dot(low, bits[j], NT)
        )

    @pl.when(leads)
    def _():
        own = [
            pltpu.make_async_copy(own_diagonal, all_diagonal.at[member], local.at[0]),
            pltpu.make_async_copy(own_link, all_link.at[member], local.at[1]),
            pltpu.make_async_copy(own_beside, all_beside.at[place], local.at[2]),
            pltpu.make_async_copy(own_corner, all_corner.at[member], local.at[3]),
        ]
        for copy in own:
            copy.start()
        all_lines[member] = own_lines[...]
        all_inverse[member] = own_inverse[...]
        all_diag[member] = own_diag[...]
        for j in range(2):
            all_half[j, member] = own_half[j]
        pl.semaphore_wait(barrier, members - 1)
        arrived(LINES, INVERSE, DIAG)
        for n in range(count):
            g, k = divmod(n, per)
            inverse = unpacked(g, k)
            plain[n] = tile(inverse)
            scaled[n] = tile(as_columns(weight(n)) * inverse * weight(n))
        for g in range(members):
            right_ref[:, pl.ds(g * share, share)] = all_lines[g, 2 * per:2 * per + 1, pl.ds(0, share)]
        arrived(FIRST)
        solve(0)
        product(0, half + EXTRA, 0)
        arrived(SECOND)
        solve(1)
        product(half + EXTRA, half, 0)
        product(half, half + EXTRA, 1)
        arrived(DIAGONAL, LINK)
        for k, other in enumerate(others):
            @pl.when(lax.div(other, members // 2) == lax.div(lead, members // 2))
            def _():
                remote(BESIDE, other, k).wait_recv()

            @pl.when(lax.rem(other, members // 2) * share < part)
            def _():
                remote(CORNER, other, k).wait_recv()

        for copy in own:
            copy.wait()


def solve_leaves(plan, arrays):
    coupling, _, _, _, _, _, parent_mat, _, link = arrays
    _, times, cells, rows, size = coupling.shape
    share, roots = link.shape[1:]
    per, members, half = times * cells, plan.members, size // 2
    count, wide = members * per, size + EXTRA
    SMEM = pl.BlockSpec(memory_space=pltpu.SMEM)
    lines = -(-(2 * per + 1) // 8) * 8
    blocks_sent = per if per % 2 else per // 2
    shape = lambda *sizes: jax.ShapeDtypeStruct(sizes, F32)
    return pl.pallas_call(
        functools.partial(leaf_kernel, plan, neighbours(plan, times, cells), per),
        out_shape=[
            shape(wide, size),
            shape(wide, count * rows),
            shape(1, size),
            shape(members, share, half // 2),
            shape(members, share, half // 2),
            shape(members // 2, share, half),
            shape(members, share, roots),
        ],
        in_specs=[VMEM, VMEM, VMEM, SMEM, VMEM, SMEM, ANY, VMEM, ANY],
        out_specs=[VMEM, VMEM, VMEM, ANY, ANY, ANY, ANY],
        scratch_shapes=[
            pltpu.VMEM((lines, LANES), F32),
            pltpu.VMEM((2, per, half, rows), F32),
            pltpu.VMEM((blocks_sent, rows, rows), F32),
            pltpu.VMEM((share, half // 2), F32),
            pltpu.VMEM((share, half // 2), F32),
            pltpu.VMEM((share, half), F32),
            pltpu.VMEM((share, roots), F32),
            pltpu.VMEM(parent_mat.shape, F32),
            pltpu.VMEM(link.shape, F32),
            pltpu.VMEM((8 * -(-per // 16), LANES), F32),
            pltpu.VMEM((members, 8 * -(-per // 16), LANES), F32),
            pltpu.VMEM((members, lines, LANES), F32),
            pltpu.VMEM((2, members, per, half, rows), F32),
            pltpu.VMEM((members, blocks_sent, rows, rows), F32),
            pltpu.VMEM((2, half + EXTRA, count * rows), F32),
            pltpu.VMEM((count, 2 * rows, 2 * rows), BF16),
            pltpu.VMEM((count, 2 * rows, 2 * rows), BF16),
            pltpu.VMEM((2, half, count * rows), BF16),
            pltpu.SemaphoreType.DMA((9,)),
            pltpu.SemaphoreType.DMA((9, members - 1)),
            pltpu.SemaphoreType.DMA((6,)),
        ],
        compiler_params=pltpu.CompilerParams(
            collective_id=0, has_side_effects=True, vmem_limit_bytes=LIMIT
        ),
    )(*arrays)


def sum_kernel(plan, term_ref, total_ref, vector_ref, strips, vectors, whole,
               send, receive):
    scen, member = plan.here()
    lead = plan.leader(scen)
    count = plan.scen
    roots = whole.shape[0]
    rows = roots // count
    barrier = pltpu.get_barrier_semaphore()

    @pl.when(member == lead)
    def _():
        peers = [lax.rem(scen + k, count) for k in range(1, count)]
        devices = [plan.device(peer, plan.leader(peer)) for peer in peers]
        for device in devices:
            pl.semaphore_signal(barrier, inc=1, device_id=device, device_id_type=MESH)
        mine = pl.ds(pl.multiple_of(scen * rows, rows), rows)
        strips[scen] = term_ref[mine, :]
        vectors[scen] = term_ref[pl.ds(roots, 8), :]
        pl.semaphore_wait(barrier, count - 1)

        def remote(kind, k, source, target):
            return pltpu.make_async_remote_copy(
                src_ref=source, dst_ref=target, send_sem=send.at[kind, k],
                recv_sem=receive.at[kind, k], device_id=devices[k], device_id_type=MESH,
            )

        copies = []
        for k, peer in enumerate(peers):
            theirs = pl.ds(pl.multiple_of(peer * rows, rows), rows)
            copies.append(remote(0, k, term_ref.at[theirs, :], strips.at[scen]))
            copies.append(remote(1, k, term_ref.at[pl.ds(roots, 8), :], vectors.at[scen]))
        for copy in copies:
            copy.start()
        for copy in copies:
            copy.wait()
        total = strips[0]
        vector = vectors[0]
        for s in range(1, count):
            total = total + strips[s]
            vector = vector + vectors[s]
        vector_ref[...] = vector
        whole[mine, :] = total
        copies = [remote(2, k, whole.at[mine, :], whole.at[mine, :]) for k in range(count - 1)]
        for copy in copies:
            copy.start()
        for copy in copies:
            copy.wait()
        total_ref[...] = whole[...]

    @pl.when(member != lead)
    def _():
        total_ref[...] = jnp.zeros_like(total_ref)
        vector_ref[...] = jnp.zeros_like(vector_ref)


def sum_terms(plan, term):
    roots = term.shape[1]
    return pl.pallas_call(
        functools.partial(sum_kernel, plan),
        out_shape=[jax.ShapeDtypeStruct((roots, roots), F32), jax.ShapeDtypeStruct((8, roots), F32)],
        in_specs=[VMEM],
        out_specs=[VMEM] * 2,
        scratch_shapes=[
            pltpu.VMEM((plan.scen, roots // plan.scen, roots), F32),
            pltpu.VMEM((plan.scen, 8, roots), F32),
            pltpu.VMEM((roots, roots), F32),
            pltpu.SemaphoreType.DMA((3, plan.scen - 1)),
            pltpu.SemaphoreType.DMA((3, plan.scen - 1)),
        ],
        compiler_params=pltpu.CompilerParams(collective_id=1, has_side_effects=True),
    )(term)


def scatter_kernel(plan, pack_ref, out_ref, landed, send, receive):
    scen, member = plan.here()
    lead = plan.leader(scen)
    barrier = pltpu.get_barrier_semaphore()

    def remote(k, other):
        return pltpu.make_async_remote_copy(
            src_ref=pack_ref.at[other], dst_ref=landed, send_sem=send.at[k],
            recv_sem=receive, device_id=plan.device(scen, other), device_id_type=MESH,
        )

    @pl.when(member != lead)
    def _():
        pl.semaphore_signal(barrier, inc=1, device_id=plan.device(scen, lead), device_id_type=MESH)
        pl.semaphore_wait(barrier, 1)
        remote(0, lead).wait_recv()
        out_ref[...] = landed[...]

    @pl.when(member == lead)
    def _():
        others = [lax.rem(lead + k, plan.members) for k in range(1, plan.members)]
        for other in others:
            pl.semaphore_signal(
                barrier, inc=1, device_id=plan.device(scen, other), device_id_type=MESH
            )
        pl.semaphore_wait(barrier, plan.members - 1)
        copies = [remote(k, other) for k, other in enumerate(others)]
        for copy in copies:
            copy.start()
        out_ref[...] = pack_ref[member]
        for copy in copies:
            copy.wait_send()


def scatter(plan, pack):
    return pl.pallas_call(
        functools.partial(scatter_kernel, plan),
        out_shape=jax.ShapeDtypeStruct(pack.shape[1:], F32),
        in_specs=[VMEM],
        out_specs=VMEM,
        scratch_shapes=[
            pltpu.VMEM(pack.shape[1:], F32),
            pltpu.SemaphoreType.DMA((plan.members - 1,)),
            pltpu.SemaphoreType.DMA,
        ],
        compiler_params=pltpu.CompilerParams(collective_id=2, has_side_effects=True),
    )(pack)


def local_call(kernel, out_shape, count, scratch=(), outside=0):
    many = isinstance(out_shape, list)
    return pl.pallas_call(
        kernel,
        out_shape=out_shape,
        in_specs=[VMEM] * (count - outside) + [ANY] * outside,
        out_specs=[VMEM] * len(out_shape) if many else VMEM,
        scratch_shapes=list(scratch),
        compiler_params=pltpu.CompilerParams(vmem_limit_bytes=LIMIT),
    )


def from_partner(block, axis, bit):
    count = lax.axis_size(axis)
    route = []
    for low in range(count):
        high = low | 1 << bit
        if high != low and high < count:
            route += [(low, high), (high, low)]
    return lax.ppermute(block, axis, route)


def neighbours(plan, times, cells):
    place = {}
    for g in range(plan.members):
        for t in range(times):
            for s in range(cells):
                at = ((g % plan.tm) * times + t, (g // plan.tm) * cells + s)
                place[at] = (g * times + t) * cells + s
    found = [None] * len(place)
    for (t, s), n in place.items():
        sides = [(t + 1, s), (t - 1, s), (t, s + 1), (t, s - 1)]
        found[n] = [place[side] for side in sides if side in place]
    return found


def body(
    plan,
    coupling,
    leaf_rhs,
    conductance,
    compressor,
    blocks,
    parent_of,
    parent_mat,
    parent_rhs,
    link,
    root_mat,
    root_rhs,
):
    _, times, cells, rows, size = coupling.shape
    per = times * cells
    roots = root_rhs.shape[0]
    share = parent_rhs.shape[1]
    schur, solved, right, corner, diagonal, beside, all_link = solve_leaves(
        plan,
        [coupling, leaf_rhs, conductance, compressor, blocks, parent_of, parent_mat, parent_rhs, link],
    )
    for bit_index in range(plan.siblings.bit_length() - 1):
        schur = schur + from_partner(schur, "scen", bit_index)
    solution_p, term = local_call(
        functools.partial(parent_kernel, plan),
        [
            jax.ShapeDtypeStruct((size, roots + LANES), F32),
            jax.ShapeDtypeStruct((roots + 8, roots), F32),
        ],
        6,
    )(
        schur,
        corner.reshape(size, size // 4),
        diagonal.reshape(size, size // 4),
        beside.reshape(size // 2, size // 2),
        right,
        all_link.reshape(size, roots),
    )
    if plan.siblings > 1:
        term = jnp.where(lax.axis_index("scen") % plan.siblings == 0, term, 0.0)
    total, vector = sum_terms(plan, term)
    width = per * rows + roots + -(-share // LANES) * LANES
    pack = local_call(
        root_kernel,
        jax.ShapeDtypeStruct((plan.members, 8, width), F32),
        6,
        [
            pltpu.VMEM(solution_p.shape, F32),
            pltpu.VMEM(solved.shape, F32),
            pltpu.SemaphoreType.DMA((2,)),
        ],
        2,
    )(root_mat, total, vector, root_rhs[None], solution_p, solved)
    shapes = [leaf_rhs.shape, (1, share), (roots,)]
    return tuple(
        local_call(finish_kernel, [jax.ShapeDtypeStruct(shape, F32) for shape in shapes], 1)(
            scatter(plan, pack)
        )
    )


def solution(mesh):
    return jax.shard_map(
        functools.partial(body, Plan(mesh)),
        mesh=mesh,
        in_specs=(
            P("scen", "tm", "space", None, None),
            P("scen", "tm", "space", None),
            P("scen", "tm", "space", None),
            P("scen", "tm", "space"),
            P("scen", "tm", "space", None, None),
            P("scen"),
            P(None, ("space", "tm"), None),
            P(None, ("space", "tm")),
            P(None, ("space", "tm"), None),
            P(),
            P(),
        ),
        out_specs=(P("scen", "tm", "space", None), P("scen", ("space", "tm")), P()),
        check_vma=False,
    )
```

```python
import functools

import jax
import jax.numpy as jnp
from jax import lax
from jax.experimental import pallas as pl
from jax.experimental.pallas import tpu as pltpu
from jax.sharding import PartitionSpec as P

PARENTS = 8
ITERS = 6
LANES = 128
F32 = jnp.float32
BF16 = jnp.bfloat16
HIGH = lax.Precision.HIGHEST
MESH = pl.DeviceIdType.MESH
VMEM = pl.BlockSpec(memory_space=pltpu.VMEM)
ANY = pl.BlockSpec(memory_space=pl.ANY)
MIB = 1024 * 1024
SETTLED = 3e-4
EXTRA = 16
NN = ((1,), (0,))
NT = ((1,), (1,))
TN = ((0,), (0,))


def full_dot(a, b, dims=NN):
    return lax.dot_general(a, b, (dims, ((), ())), precision=HIGH, preferred_element_type=F32)


def fast_dot(a, b, dims=NN):
    return lax.dot_general(a, b, (dims, ((), ())), preferred_element_type=F32)


def halves(x):
    top = x.astype(BF16)
    return top, (x - top.astype(F32)).astype(BF16)


def as_columns(row):
    return jnp.broadcast_to(row, (LANES, LANES)).T


def near_dot(a, b, dims=NN):
    a_top, a_low = halves(a)
    b_top, b_low = halves(b)
    return fast_dot(a_top, b_top, dims) + fast_dot(a_top, b_low, dims) + fast_dot(a_low, b_top, dims)


def spd_inverse(matrix, steps=None):
    size = matrix.shape[0]
    row = lax.broadcasted_iota(jnp.int32, (size, size), 0)
    column = lax.broadcasted_iota(jnp.int32, (size, size), 1)
    identity = jnp.where(row == column, 1.0, 0.0).astype(F32)
    square = near_dot(matrix, matrix)
    plain = jnp.max(jnp.sum(jnp.abs(matrix), axis=0, keepdims=True), axis=1, keepdims=True)
    squared = jnp.max(jnp.sum(jnp.abs(square), axis=0, keepdims=True), axis=1, keepdims=True)
    bound = jnp.maximum(jnp.minimum(plain, jnp.sqrt(squared)) * 1.0001, 1.0)
    total, spread = bound + 1.0, bound - 1.0
    scale = 1.0 / (2.0 * total * total - spread * spread)
    alpha, beta = 8.0 * total * scale, 8.0 * scale
    start = alpha * identity - beta * matrix
    residual = identity - alpha * matrix + beta * square

    def grow(x, r):
        both = near_dot(jnp.concatenate([x, r], axis=0), r)
        return x + both[:size], both[size:]

    def correct(_, x):
        left = identity - full_dot(matrix, x)
        return x + fast_dot(x.astype(BF16), left.astype(BF16))

    if steps is not None:
        x, _ = lax.fori_loop(0, steps, lambda _, state: grow(*state), (start, residual))
        return lax.fori_loop(0, 2, correct, x)
    rho = jnp.max(spread * spread * scale)
    largest = jnp.max(bound)
    _, _, x, _ = lax.while_loop(
        lambda state: (state[0] > SETTLED) & (state[1] < 32),
        lambda state: (state[0] * state[0], state[1] + 1) + grow(*state[2:]),
        (rho, jnp.int32(0), start, residual),
    )
    rounds = 1 + (largest > 50.0).astype(jnp.int32) + (largest > 1000.0).astype(jnp.int32)
    return lax.fori_loop(0, rounds, correct, x)


def steps_for(bound):
    rho = (bound - 1.0) ** 2 / (2.0 * (bound + 1.0) ** 2 - (bound - 1.0) ** 2)
    steps = 0
    while rho > SETTLED:
        rho, steps = rho * rho, steps + 1
    return steps


def parent_kernel(plan, schur_ref, corner_ref, diagonal_ref, beside_ref, right_ref, link_ref,
                  solution_ref, term_ref):
    part = diagonal_ref.shape[1]
    half = 2 * part
    size = 2 * half
    roots = link_ref.shape[1]
    scen, _ = plan.here()
    near = lax.div(plan.leader(scen), plan.members // 2)
    reduced = schur_ref[pl.ds(half, 8), :][0:1] - right_ref[...]
    right = jnp.concatenate(
        [as_columns(reduced[:, c:c + LANES]) for c in range(0, size, LANES)], axis=0
    )
    a, b = pl.ds(0, half), pl.ds(half, half)
    behind = pl.ds(half + EXTRA, half)
    sides = jnp.concatenate([link_ref[...], right], axis=1)
    beside = beside_ref[...]

    def diagonal(start):
        upper = jnp.concatenate(
            [corner_ref[pl.ds(start, part), :], diagonal_ref[pl.ds(start, part), :]], axis=1
        )
        lower = jnp.concatenate(
            [upper[:, part:].T, diagonal_ref[pl.ds(start + part, part), :]], axis=1
        )
        return jnp.concatenate([upper, lower], axis=0)

    h11 = diagonal(0) + schur_ref[a, a]
    h21 = jnp.where(near == 0, beside.T, beside) + schur_ref[behind, a]
    h22 = diagonal(half) + schur_ref[behind, b]
    x11 = spd_inverse(h11)
    across = full_dot(x11, h21, NT)
    ahead = near_dot(x11, sides[:half])
    x22 = spd_inverse(h22 - full_dot(h21, across))
    lower = near_dot(x22, sides[half:] - near_dot(h21, ahead))
    upper = ahead - near_dot(across, lower)
    solution_ref[a, :] = upper
    solution_ref[b, :] = lower
    term_ref[...] = near_dot(solution_ref[...], link_ref[...], TN)[:roots + 8]


def root_kernel(matrix_ref, term_ref, vector_ref, right_ref, solution_any, solved_any, pack_ref,
                solution_ref, solved_ref, local):
    loads = [
        pltpu.make_async_copy(solution_any, solution_ref, local.at[0]),
        pltpu.make_async_copy(solved_any, solved_ref, local.at[1]),
    ]
    for load in loads:
        load.start()
    roots = matrix_ref.shape[0]
    size = solution_ref.shape[0]
    groups = pack_ref.shape[0]
    half = size // 2
    width = solved_ref.shape[1] // groups
    share = size // groups
    inverse = spd_inverse(matrix_ref[...] + term_ref[...])
    root = full_dot(right_ref[...] - vector_ref[...], inverse)
    for load in loads:
        load.wait()
    lane = lax.broadcasted_iota(jnp.int32, (8, LANES), 1)
    unit = jnp.where(lane == 0, 1.0, 0.0).astype(F32)
    parent = full_dot(jnp.concatenate([root, unit], axis=1), solution_ref[...], NT)
    leaf = (
        solved_ref[pl.ds(half, 8), :]
        - near_dot(parent[:, :half], solved_ref[pl.ds(0, half), :])
        - near_dot(parent[:, half:], solved_ref[pl.ds(half + EXTRA, half), :])
    )
    for g in range(groups):
        pack_ref[g, :, pl.ds(0, width)] = leaf[:, g * width:(g + 1) * width]
        pack_ref[g, :, pl.ds(width, roots)] = root
        pack_ref[g, :, pl.ds(width + roots, share)] = parent[:, g * share:(g + 1) * share]


def finish_kernel(line_ref, leaf_ref, parent_ref, root_ref):
    times, cells = leaf_ref.shape[1:3]
    roots, share = root_ref.shape[0], parent_ref.shape[1]
    base = times * cells * LANES
    for k in range(times * cells):
        t, c = divmod(k, cells)
        leaf_ref[0, t, c:c + 1, :] = line_ref[0:1, pl.ds(k * LANES, LANES)]
    root_ref[...] = line_ref[0, pl.ds(base, roots)]
    parent_ref[...] = line_ref[0:1, pl.ds(base + roots, share)]


class Plan:
    def __init__(self, mesh):
        self.scen, self.space, self.tm = (mesh.shape[name] for name in ("scen", "space", "tm"))
        self.members = self.space * self.tm
        self.siblings = self.scen // PARENTS

    def leader(self, scen):
        middle = self.members // 2
        if self.siblings == 1:
            return middle - lax.rem(scen, 2)
        return middle + 0 * scen

    def device(self, scen, member):
        return (scen, lax.div(member, self.tm), lax.rem(member, self.tm))

    def here(self):
        return lax.axis_index("scen"), lax.axis_index("space") * self.tm + lax.axis_index("tm")


def leaf_kernel(plan, beside, per, coupling_ref, rhs_ref, conductance_ref, compressor_ref, blocks_ref,
                parent_of_ref, parent_mat_ref, parent_rhs_ref, link_ref,
                schur_ref, solved_ref, right_ref, all_corner, all_diagonal, all_beside, all_link,
                own_lines, own_half, own_inverse, own_corner, own_diagonal, own_beside, own_link,
                mats, links, own_diag, all_diag,
                all_lines, all_half, all_inverse,
                field, plain, scaled, bits, send, receive, local):
    count = len(beside)
    members = plan.members
    packed = per % 2 == 0
    times, cells = coupling_ref.shape[1:3]
    half = coupling_ref.shape[-1] // 2
    share = parent_rhs_ref.shape[1]
    scen, member = plan.here()
    lead = plan.leader(scen)
    leads = member == lead
    close = lax.div(member, members // 2) == lax.div(lead, members // 2)
    place = lax.rem(member, members // 2)
    barrier = pltpu.get_barrier_semaphore()
    LINES, FIRST, INVERSE, SECOND, DIAGONAL, LINK, BESIDE, CORNER, DIAG = range(9)
    part = half // 2
    cornered = place * share < part
    loads = [
        pltpu.make_async_copy(parent_mat_ref, mats, local.at[4]),
        pltpu.make_async_copy(link_ref, links, local.at[5]),
    ]
    for load in loads:
        load.start()

    def remote(kind, at, slot):
        source, target = {
            LINES: (own_lines, all_lines.at[at]),
            FIRST: (own_half.at[0], all_half.at[0, at]),
            INVERSE: (own_inverse, all_inverse.at[at]),
            SECOND: (own_half.at[1], all_half.at[1, at]),
            DIAGONAL: (own_diagonal, all_diagonal.at[at]),
            CORNER: (own_corner, all_corner.at[at]),
            DIAG: (own_diag, all_diag.at[at]),
            LINK: (own_link, all_link.at[at]),
            BESIDE: (own_beside, all_beside.at[lax.rem(at, members // 2)]),
        }[kind]
        return pltpu.make_async_remote_copy(
            src_ref=source, dst_ref=target, send_sem=send.at[kind], recv_sem=receive.at[kind, slot],
            device_id=plan.device(scen, lead), device_id_type=MESH,
        )

    others = [lax.rem(lead + k, members) for k in range(1, members)]
    slot = lax.rem(member - lead + members, members) - 1

    @pl.when(leads)
    def _():
        for other in others:
            pl.semaphore_signal(
                barrier, inc=1, device_id=plan.device(scen, other), device_id_type=MESH
            )

    @pl.when(jnp.logical_not(leads))
    def _():
        pl.semaphore_signal(barrier, inc=1, device_id=plan.device(scen, lead), device_id_type=MESH)

    label = parent_of_ref[0]
    own_lines[...] = jnp.zeros_like(own_lines)
    own_diag[...] = jnp.zeros_like(own_diag)
    for k in range(per):
        t, c = divmod(k, cells)
        own_lines[k:k + 1, :] = rhs_ref[0, t, c:c + 1, :]
        doubled = 1.0 + compressor_ref[0, t, c].astype(F32)
        own_lines[per + k:per + k + 1, :] = conductance_ref[0, t, c:c + 1, :] * doubled * 0.5
        for j in range(2):
            own_half[j, k] = coupling_ref[0, t, c, :, pl.ds(j * half, half)].astype(F32).T
    own_lines[2 * per:2 * per + 1, pl.ds(0, share)] = parent_rhs_ref[pl.ds(label, 1), :]

    @pl.when(jnp.logical_not(leads))
    def _():
        pl.semaphore_wait(barrier, 1)
        remote(LINES, member, slot).start()
        remote(FIRST, member, slot).start()

    rows = blocks_ref.shape[-1]
    zero = jnp.zeros((rows, rows), F32)
    for i in range(0, per, 2):
        j = min(i + 1, per - 1)
        first = blocks_ref[0, i // cells, i % cells]
        second = blocks_ref[0, j // cells, j % cells]
        pair = jnp.concatenate(
            [jnp.concatenate([first, zero], axis=1), jnp.concatenate([zero, second], axis=1)], axis=0
        )
        found = spd_inverse(pair, steps_for(8.0 * rows))
        if packed:
            row = lax.broadcasted_iota(jnp.int32, (rows, rows), 0)
            column = lax.broadcasted_iota(jnp.int32, (rows, rows), 1)
            own_inverse[i // 2] = jnp.where(row <= column, found[:rows, :rows], found[rows:, rows:])
            kept = jnp.where(row == column, found[rows:, rows:], 0.0)
            own_diag[i // 2:i // 2 + 1, :] = jnp.sum(kept, axis=0, keepdims=True)
        else:
            own_inverse[i] = found[:rows, :rows]
            own_inverse[j] = found[rows:, rows:]
    for load in loads:
        load.wait()
    strip = mats[label]
    lower = lax.div(member, members // 2) == 0
    square = jnp.where(lower, strip[:, :half], strip[:, half:])
    own_corner[...] = square[:, :part]
    own_diagonal[...] = square[:, part:]
    own_beside[...] = jnp.where(lower, strip[:, half:], strip[:, :half])
    own_link[...] = links[label]

    @pl.when(jnp.logical_not(leads))
    def _():
        remote(INVERSE, member, slot).start()
        remote(DIAG, member, slot).start()
        remote(SECOND, member, slot).start()
        for kind in (LINES, FIRST, INVERSE, DIAG, SECOND):
            remote(kind, member, slot).wait_send()
        remote(DIAGONAL, member, slot).start()
        remote(LINK, member, slot).start()

        @pl.when(cornered)
        def _():
            remote(CORNER, member, slot).start()
            remote(CORNER, member, slot).wait_send()

        @pl.when(close)
        def _():
            remote(BESIDE, member, slot).start()
            remote(BESIDE, member, slot).wait_send()

        remote(DIAGONAL, member, slot).wait_send()
        remote(LINK, member, slot).wait_send()

    def arrived(*kinds):
        for kind in kinds:
            for k, other in enumerate(others):
                remote(kind, other, k).wait_recv()

    def unpacked(g, k):
        if not packed:
            return all_inverse[g, k]
        both = all_inverse[g, k // 2]
        other = both.T
        row = lax.broadcasted_iota(jnp.int32, both.shape, 0)
        column = lax.broadcasted_iota(jnp.int32, both.shape, 1)
        if k % 2 == 0:
            return jnp.where(row <= column, both, other)
        middle = jnp.broadcast_to(all_diag[g, k // 2:k // 2 + 1, :], both.shape)
        return jnp.where(row > column, both, jnp.where(row < column, other, middle))

    def tile(matrix):
        top, low = halves(matrix)
        return jnp.concatenate(
            [
                jnp.concatenate([top, low], axis=1),
                jnp.concatenate([top, jnp.zeros_like(top)], axis=1),
            ],
            axis=0,
        )

    def apply(x, matrix):
        both = fast_dot(jnp.concatenate(halves(x), axis=1), matrix)
        return both[:, :LANES] + both[:, LANES:]

    def source(j, n):
        g, k = divmod(n, per)
        if j == 1:
            return all_half[j, g, k]
        right = jnp.broadcast_to(all_lines[g, k:k + 1, :], (EXTRA, LANES))
        return jnp.concatenate([all_half[j, g, k], right], axis=0)

    def weight(n):
        g, k = divmod(n, per)
        return all_lines[g, per + k:per + k + 1, :]

    def lanes(n):
        return pl.ds(n * LANES, LANES)

    def around(at, n, width):
        total = field[at, pl.ds(0, width), lanes(beside[n][0])]
        for m in beside[n][1:]:
            total = total + field[at, pl.ds(0, width), lanes(m)]
        return total

    last = (ITERS - 2) % 2

    def solve(j):
        start, width = (half + EXTRA, half) if j else (0, half + EXTRA)
        here, top = pl.ds(start, width), pl.ds(0, width)
        for n in range(count):
            g, k = divmod(n, per)
            bits[j, :, lanes(n)] = all_half[j, g, k].astype(BF16)
            first = weight(n) * apply(source(j, n), plain[n])
            field[0, top, lanes(n)] = first
            solved_ref[here, lanes(n)] = first

        def sweep(k, carry):
            now = lax.rem(k, 2)
            for n in range(count):
                moved = apply(around(now, n, width), scaled[n])
                field[1 - now, top, lanes(n)] = solved_ref[here, lanes(n)] + moved
            return carry

        lax.fori_loop(0, ITERS - 2, sweep, 0)
        for n in range(count):
            drive = source(j, n) + weight(n) * around(last, n, width)
            solved_ref[here, lanes(n)] = apply(drive, plain[n])

    def product(start, width, j):
        top, low = halves(solved_ref[pl.ds(start, width), :])
        schur_ref[pl.ds(start, width), pl.ds(j * half, half)] = (
            fast_dot(top, bits[j], NT) + fast_dot(low, bits[j], NT)
        )

    @pl.when(leads)
    def _():
        own = [
            pltpu.make_async_copy(own_diagonal, all_diagonal.at[member], local.at[0]),
            pltpu.make_async_copy(own_link, all_link.at[member], local.at[1]),
            pltpu.make_async_copy(own_beside, all_beside.at[place], local.at[2]),
            pltpu.make_async_copy(own_corner, all_corner.at[member], local.at[3]),
        ]
        for copy in own:
            copy.start()
        all_lines[member] = own_lines[...]
        all_inverse[member] = own_inverse[...]
        all_diag[member] = own_diag[...]
        for j in range(2):
            all_half[j, member] = own_half[j]
        pl.semaphore_wait(barrier, members - 1)
        arrived(LINES, INVERSE, DIAG)
        for n in range(count):
            g, k = divmod(n, per)
            inverse = unpacked(g, k)
            plain[n] = tile(inverse)
            scaled[n] = tile(as_columns(weight(n)) * inverse * weight(n))
        for g in range(members):
            right_ref[:, pl.ds(g * share, share)] = all_lines[g, 2 * per:2 * per + 1, pl.ds(0, share)]
        arrived(FIRST)
        solve(0)
        product(0, half + EXTRA, 0)
        arrived(SECOND)
        solve(1)
        product(half + EXTRA, half, 0)
        product(half, half + EXTRA, 1)
        arrived(DIAGONAL, LINK)
        for k, other in enumerate(others):
            @pl.when(lax.div(other, members // 2) == lax.div(lead, members // 2))
            def _():
                remote(BESIDE, other, k).wait_recv()

            @pl.when(lax.rem(other, members // 2) * share < part)
            def _():
                remote(CORNER, other, k).wait_recv()

        for copy in own:
            copy.wait()


def solve_leaves(plan, arrays):
    coupling, _, _, _, _, _, parent_mat, _, link = arrays
    _, times, cells, rows, size = coupling.shape
    share, roots = link.shape[1:]
    per, members, half = times * cells, plan.members, size // 2
    count, wide = members * per, size + EXTRA
    SMEM = pl.BlockSpec(memory_space=pltpu.SMEM)
    lines = -(-(2 * per + 1) // 8) * 8
    blocks_sent = per if per % 2 else per // 2
    shape = lambda *sizes: jax.ShapeDtypeStruct(sizes, F32)
    return pl.pallas_call(
        functools.partial(leaf_kernel, plan, neighbours(plan, times, cells), per),
        out_shape=[
            shape(wide, size),
            shape(wide, count * rows),
            shape(1, size),
            shape(members, share, half // 2),
            shape(members, share, half // 2),
            shape(members // 2, share, half),
            shape(members, share, roots),
        ],
        in_specs=[VMEM, VMEM, VMEM, SMEM, VMEM, SMEM, ANY, VMEM, ANY],
        out_specs=[VMEM, VMEM, VMEM, ANY, ANY, ANY, ANY],
        scratch_shapes=[
            pltpu.VMEM((lines, LANES), F32),
            pltpu.VMEM((2, per, half, rows), F32),
            pltpu.VMEM((blocks_sent, rows, rows), F32),
            pltpu.VMEM((share, half // 2), F32),
            pltpu.VMEM((share, half // 2), F32),
            pltpu.VMEM((share, half), F32),
            pltpu.VMEM((share, roots), F32),
            pltpu.VMEM(parent_mat.shape, F32),
            pltpu.VMEM(link.shape, F32),
            pltpu.VMEM((8 * -(-per // 16), LANES), F32),
            pltpu.VMEM((members, 8 * -(-per // 16), LANES), F32),
            pltpu.VMEM((members, lines, LANES), F32),
            pltpu.VMEM((2, members, per, half, rows), F32),
            pltpu.VMEM((members, blocks_sent, rows, rows), F32),
            pltpu.VMEM((2, half + EXTRA, count * rows), F32),
            pltpu.VMEM((count, 2 * rows, 2 * rows), BF16),
            pltpu.VMEM((count, 2 * rows, 2 * rows), BF16),
            pltpu.VMEM((2, half, count * rows), BF16),
            pltpu.SemaphoreType.DMA((9,)),
            pltpu.SemaphoreType.DMA((9, members - 1)),
            pltpu.SemaphoreType.DMA((6,)),
        ],
        compiler_params=pltpu.CompilerParams(
            collective_id=0,
            has_side_effects=True,
            vmem_limit_bytes=(28 if count <= 8 else 56) * MIB,
        ),
    )(*arrays)


def sum_kernel(plan, term_ref, total_ref, vector_ref, strips, vectors, whole,
               send, receive):
    scen, member = plan.here()
    lead = plan.leader(scen)
    count = plan.scen
    roots = whole.shape[0]
    rows = roots // count
    barrier = pltpu.get_barrier_semaphore()

    @pl.when(member == lead)
    def _():
        peers = [lax.rem(scen + k, count) for k in range(1, count)]
        devices = [plan.device(peer, plan.leader(peer)) for peer in peers]
        for device in devices:
            pl.semaphore_signal(barrier, inc=1, device_id=device, device_id_type=MESH)
        mine = pl.ds(pl.multiple_of(scen * rows, rows), rows)
        strips[scen] = term_ref[mine, :]
        vectors[scen] = term_ref[pl.ds(roots, 8), :]
        pl.semaphore_wait(barrier, count - 1)

        def remote(kind, k, source, target):
            return pltpu.make_async_remote_copy(
                src_ref=source, dst_ref=target, send_sem=send.at[kind, k],
                recv_sem=receive.at[kind, k], device_id=devices[k], device_id_type=MESH,
            )

        copies = []
        for k, peer in enumerate(peers):
            theirs = pl.ds(pl.multiple_of(peer * rows, rows), rows)
            copies.append(remote(0, k, term_ref.at[theirs, :], strips.at[scen]))
            copies.append(remote(1, k, term_ref.at[pl.ds(roots, 8), :], vectors.at[scen]))
        for copy in copies:
            copy.start()
        for copy in copies:
            copy.wait()
        total = strips[0]
        vector = vectors[0]
        for s in range(1, count):
            total = total + strips[s]
            vector = vector + vectors[s]
        vector_ref[...] = vector
        whole[mine, :] = total
        copies = [remote(2, k, whole.at[mine, :], whole.at[mine, :]) for k in range(count - 1)]
        for copy in copies:
            copy.start()
        for copy in copies:
            copy.wait()
        total_ref[...] = whole[...]

    @pl.when(member != lead)
    def _():
        total_ref[...] = jnp.zeros_like(total_ref)
        vector_ref[...] = jnp.zeros_like(vector_ref)


def sum_terms(plan, term):
    roots = term.shape[1]
    return pl.pallas_call(
        functools.partial(sum_kernel, plan),
        out_shape=[jax.ShapeDtypeStruct((roots, roots), F32), jax.ShapeDtypeStruct((8, roots), F32)],
        in_specs=[VMEM],
        out_specs=[VMEM] * 2,
        scratch_shapes=[
            pltpu.VMEM((plan.scen, roots // plan.scen, roots), F32),
            pltpu.VMEM((plan.scen, 8, roots), F32),
            pltpu.VMEM((roots, roots), F32),
            pltpu.SemaphoreType.DMA((3, plan.scen - 1)),
            pltpu.SemaphoreType.DMA((3, plan.scen - 1)),
        ],
        compiler_params=pltpu.CompilerParams(collective_id=1, has_side_effects=True),
    )(term)


def scatter_kernel(plan, pack_ref, out_ref, landed, send, receive):
    scen, member = plan.here()
    lead = plan.leader(scen)
    barrier = pltpu.get_barrier_semaphore()

    def remote(k, other):
        return pltpu.make_async_remote_copy(
            src_ref=pack_ref.at[other], dst_ref=landed, send_sem=send.at[k],
            recv_sem=receive, device_id=plan.device(scen, other), device_id_type=MESH,
        )

    @pl.when(member != lead)
    def _():
        pl.semaphore_signal(barrier, inc=1, device_id=plan.device(scen, lead), device_id_type=MESH)
        pl.semaphore_wait(barrier, 1)
        remote(0, lead).wait_recv()
        out_ref[...] = landed[...]

    @pl.when(member == lead)
    def _():
        others = [lax.rem(lead + k, plan.members) for k in range(1, plan.members)]
        for other in others:
            pl.semaphore_signal(
                barrier, inc=1, device_id=plan.device(scen, other), device_id_type=MESH
            )
        pl.semaphore_wait(barrier, plan.members - 1)
        copies = [remote(k, other) for k, other in enumerate(others)]
        for copy in copies:
            copy.start()
        out_ref[...] = pack_ref[member]
        for copy in copies:
            copy.wait_send()


def scatter(plan, pack):
    return pl.pallas_call(
        functools.partial(scatter_kernel, plan),
        out_shape=jax.ShapeDtypeStruct(pack.shape[1:], F32),
        in_specs=[VMEM],
        out_specs=VMEM,
        scratch_shapes=[
            pltpu.VMEM(pack.shape[1:], F32),
            pltpu.SemaphoreType.DMA((plan.members - 1,)),
            pltpu.SemaphoreType.DMA,
        ],
        compiler_params=pltpu.CompilerParams(collective_id=2, has_side_effects=True),
    )(pack)


def local_call(kernel, out_shape, count, scratch=(), outside=0, limit=24 * MIB):
    many = isinstance(out_shape, list)
    return pl.pallas_call(
        kernel,
        out_shape=out_shape,
        in_specs=[VMEM] * (count - outside) + [ANY] * outside,
        out_specs=[VMEM] * len(out_shape) if many else VMEM,
        scratch_shapes=list(scratch),
        compiler_params=pltpu.CompilerParams(vmem_limit_bytes=limit),
    )


def from_partner(block, axis, bit):
    count = lax.axis_size(axis)
    route = []
    for low in range(count):
        high = low | 1 << bit
        if high != low and high < count:
            route += [(low, high), (high, low)]
    return lax.ppermute(block, axis, route)


def neighbours(plan, times, cells):
    place = {}
    for g in range(plan.members):
        for t in range(times):
            for s in range(cells):
                at = ((g % plan.tm) * times + t, (g // plan.tm) * cells + s)
                place[at] = (g * times + t) * cells + s
    found = [None] * len(place)
    for (t, s), n in place.items():
        sides = [(t + 1, s), (t - 1, s), (t, s + 1), (t, s - 1)]
        found[n] = [place[side] for side in sides if side in place]
    return found


def body(
    plan,
    coupling,
    leaf_rhs,
    conductance,
    compressor,
    blocks,
    parent_of,
    parent_mat,
    parent_rhs,
    link,
    root_mat,
    root_rhs,
):
    _, times, cells, rows, size = coupling.shape
    per = times * cells
    roots = root_rhs.shape[0]
    share = parent_rhs.shape[1]
    schur, solved, right, corner, diagonal, beside, all_link = solve_leaves(
        plan,
        [coupling, leaf_rhs, conductance, compressor, blocks, parent_of, parent_mat, parent_rhs, link],
    )
    for bit_index in range(plan.siblings.bit_length() - 1):
        schur = schur + from_partner(schur, "scen", bit_index)
    solution_p, term = local_call(
        functools.partial(parent_kernel, plan),
        [
            jax.ShapeDtypeStruct((size, roots + LANES), F32),
            jax.ShapeDtypeStruct((roots + 8, roots), F32),
        ],
        6,
    )(
        schur,
        corner.reshape(size, size // 4),
        diagonal.reshape(size, size // 4),
        beside.reshape(size // 2, size // 2),
        right,
        all_link.reshape(size, roots),
    )
    if plan.siblings > 1:
        term = jnp.where(lax.axis_index("scen") % plan.siblings == 0, term, 0.0)
    total, vector = sum_terms(plan, term)
    width = per * rows + roots + -(-share // LANES) * LANES
    pack = local_call(
        root_kernel,
        jax.ShapeDtypeStruct((plan.members, 8, width), F32),
        6,
        [
            pltpu.VMEM(solution_p.shape, F32),
            pltpu.VMEM(solved.shape, F32),
            pltpu.SemaphoreType.DMA((2,)),
        ],
        2,
        (16 if plan.members <= 4 else 32) * MIB,
    )(root_mat, total, vector, root_rhs[None], solution_p, solved)
    shapes = [leaf_rhs.shape, (1, share), (roots,)]
    return tuple(
        local_call(finish_kernel, [jax.ShapeDtypeStruct(shape, F32) for shape in shapes], 1)(
            scatter(plan, pack)
        )
    )


def solution(mesh):
    return jax.shard_map(
        functools.partial(body, Plan(mesh)),
        mesh=mesh,
        in_specs=(
            P("scen", "tm", "space", None, None),
            P("scen", "tm", "space", None),
            P("scen", "tm", "space", None),
            P("scen", "tm", "space"),
            P("scen", "tm", "space", None, None),
            P("scen"),
            P(None, ("space", "tm"), None),
            P(None, ("space", "tm")),
            P(None, ("space", "tm"), None),
            P(),
            P(),
        ),
        out_specs=(P("scen", "tm", "space", None), P("scen", ("space", "tm")), P()),
        check_vma=False,
    )
```
